256 devices in a mesh: band: 64 (over y, z, core), lev: 4 (over x).
Axes of the slice: x: 4, y: 4, z: 8, core: 2. Of those that a mesh axis runs over, the one named last changes fastest.
Arguments:
- arrival_adj: bfloat16 [4, 16, 1280, 2560], P(None, None, ('band', 'lev')), may hold values from -6 to 6
- block_weights: bfloat16 [64, 4, 100, 128, 128], P('band', 'lev'), may hold values from -0.5 to 0.5
- dest_band: int32 [64, 4, 100], P('band', 'lev'), may hold values from 0 to 63, as said below
- dest_block: int32 [64, 4, 100], P('band', 'lev'), may hold values from 0 to 99, as said below
- lower_coef: float32 [4, 16], replicated, may hold values from 0.05 to 4
- upper_coef: float32 [4, 16], replicated, may hold values from 0.05 to 4
- order_pairs: int32 [64], replicated, may hold values from 0 to 63, each once
- legendre: bfloat16 [64, 1280, 1281], P('band'), may hold values from -0.15625 to 0.15625
Outputs:
- grid_adj: float32 [4, 16, 1280, 2560], P(None, None, ('band', 'lev'))
- spectral: float32 [64, 1281, 2, 64], P('band', None, None, 'lev')
The draws below stay inside these ranges and needn't reach their ends.
Inputs may be any that keep to these rules, and one draw needn't show every extreme that they name: `dest_band`: A slot's target band lies within 2 bands of its own band; no device has more than 40 slots naming one band, and some device has exactly that many. In every latitude group, each column block of each band is named (by dest_band and dest_block together) by exactly one slot over all devices of the group. `order_pairs`: each pair slot names a different lower order; the pair stands for orders m and 1279 - m.
All inputs are finite; a program needn't handle non-finite values.
Results may differ from the reference program's by a relative error of at most 0.0041.
Values may be sent and summed in bfloat16 or wider, within the bound.
No kernel may reach another device: no remote copies, remote signals or barrier semaphores. Data moves between devices by JAX's collectives and lax.ppermute only.
A program may use at most 128 MiB of HBM per device.

```python
import math
import jax
import jax.numpy as jnp
from jax import lax

FIELDS = 4
LEVELS = 16
FEATURES = 64
LONGITUDES = 2560
ORDERS = 1280
LAT_DEV = 5
BAND_COUNT = 64
SEGMENT_COUNT = 4
LATITUDES = 1280
PAIR_COUNT = 64
BLOCK_COLS = 128
BLOCK_ROWS = 128
BAND_REACH = 2
BLOCKS_DEV = 100
SLOTS_DEV = 100


def pair_odd(bands):
    odd = bands % 2 == 1
    upward = odd & (bands + 1 < BAND_COUNT)
    downward = ~odd & (bands > 0)
    return jnp.where(upward, bands + 1, jnp.where(downward, bands - 1, bands))


def route_tables(key):
    key_group = jax.random.fold_in(key, 101)
    key_block = jax.random.fold_in(key, 202)
    group_count = 2 * BAND_REACH + 1
    group_size = SLOTS_DEV // group_count
    slot_ids = jnp.arange(SLOTS_DEV, dtype=jnp.int32)
    bands = jnp.arange(BAND_COUNT, dtype=jnp.int32)
    swap_even = jnp.bitwise_xor(bands, 1)
    swap_odd = pair_odd(bands)
    images = jnp.stack([bands, swap_even, swap_odd, jnp.bitwise_xor(swap_odd, 1), pair_odd(swap_even)], axis=0)
    scores = jax.random.randint(key_group, (SEGMENT_COUNT, SLOTS_DEV), 0, 1 << 20) * SLOTS_DEV + slot_ids[None, :]
    order = jnp.argsort(scores, axis=-1, stable=True)
    rank = jnp.argsort(order, axis=-1, stable=True).astype(jnp.int32)
    lane_group = rank // group_size
    targets = images[lane_group[None, :, :], bands[:, None, None]]
    block_scores = jax.random.randint(key_block, (BAND_COUNT, SEGMENT_COUNT, SLOTS_DEV), 0, 1 << 20) * SLOTS_DEV + slot_ids[None, None, :]
    sigma = jnp.argsort(block_scores, axis=-1, stable=True).astype(jnp.int32)
    segments = jnp.arange(SEGMENT_COUNT, dtype=jnp.int32)[None, :, None]
    blocks = sigma[targets, segments, slot_ids[None, None, :]]
    return (targets.astype(jnp.int32), blocks.astype(jnp.int32))


def draw_dest_band(key, part):
    return route_tables(key)[0]


def draw_dest_block(key, part):
    return route_tables(key)[1]


def shard_levels(rng, shape, split, low, high):
    def one(axis_at, parts):
        draws = jax.random.uniform(jax.random.fold_in(jax.random.fold_in(rng, 6), axis_at), (parts,), jnp.float32, low / len(split), high / len(split))
        return jnp.repeat(jnp.exp(draws), shape[axis_at] // parts).reshape((-1,) + (1,) * (len(shape) - axis_at - 1))

    level = one(*split[0])
    for cut in split[1:]:
        level = level * one(*cut)
    return level


def noise(stream_key, dims, deviation, most, shards=(), held_as=jnp.bfloat16):
    array = deviation * jax.random.normal(stream_key, dims, jnp.float32)
    if shards:
        array = array * shard_levels(stream_key, dims, shards, -0.22, 0.18)
    return jnp.clip(array, -most, most).astype(held_as)


def setup_inputs(seed: int = 0) -> dict:
    key_list = jax.random.split(jax.random.key(seed), 9)
    return {
        "arrival_adj": noise(key_list[0], (FIELDS, LEVELS, LATITUDES, LONGITUDES), 1.0, 6.0, ((2, 256),)),
        "block_weights": noise(key_list[1], (BAND_COUNT, SEGMENT_COUNT, SLOTS_DEV, BLOCK_ROWS, BLOCK_COLS), BLOCK_ROWS ** -0.5, 0.5, ((0, 64), (1, 4))),
        "dest_band": draw_dest_band(jax.random.fold_in(key_list[8], 71), 0),
        "dest_block": draw_dest_block(jax.random.fold_in(key_list[8], 71), 0),
        "lower_coef": jnp.clip(jnp.exp(jax.random.uniform(key_list[4], (FIELDS, LEVELS), jnp.float32, math.log(0.05), math.log(4.0))), 0.05, 4.0),
        "upper_coef": jnp.clip(jnp.exp(jax.random.uniform(key_list[5], (FIELDS, LEVELS), jnp.float32, math.log(0.05), math.log(4.0))), 0.05, 4.0),
        "order_pairs": jax.random.permutation(key_list[6], PAIR_COUNT).astype(jnp.int32),
        "legendre": noise(key_list[7], (PAIR_COUNT, LATITUDES, ORDERS + 1), LATITUDES ** -0.5, 0.15625, ((0, 64),)),
    }


def fourier_table(order_pairs):
    paired = jnp.stack([order_pairs, ORDERS - 1 - order_pairs], axis=1).reshape(-1)
    positions = jnp.arange(LONGITUDES, dtype=jnp.int32)
    phase = positions[:, None] * paired[None, :] % LONGITUDES
    angle = phase.astype(jnp.float32) * (2.0 * math.pi / LONGITUDES)
    factor = 1.0 / math.sqrt(LONGITUDES)
    table = jnp.stack([jnp.cos(angle) * factor, -jnp.sin(angle) * factor], axis=-1)
    return table.reshape(LONGITUDES, paired.shape[0] * 2)

def vertical_operator(lower_coef, upper_coef):
    diagonal = 1.0 + lower_coef + upper_coef
    edge = jnp.zeros((lower_coef.shape[0], 1), lower_coef.dtype)
    below = jnp.concatenate([edge, -upper_coef[:, :-1]], axis=1)
    above = jnp.concatenate([-lower_coef[:, 1:], edge], axis=1)
    return (below, diagonal, above)

def reference(arrival_adj, block_weights, dest_band, dest_block, lower_coef, upper_coef, order_pairs, legendre):
    columns = LAT_DEV * LONGITUDES
    grid_in = arrival_adj.reshape(FEATURES, BAND_COUNT, SEGMENT_COUNT, columns).transpose(1, 2, 0, 3)
    grid_in = grid_in.reshape(BAND_COUNT, SEGMENT_COUNT, FEATURES, SLOTS_DEV, BLOCK_ROWS)
    segment_ids = jnp.arange(SEGMENT_COUNT, dtype=jnp.int32)[:, None]
    drop_index = BAND_COUNT * SEGMENT_COUNT * BLOCKS_DEV

    def band_step(totals, slices):
        rows_in, weights, targets, target_blocks = slices
        payload = jnp.einsum('sfja,sjac->sjfc', rows_in.astype(jnp.float32), weights.astype(jnp.float32)).astype(jnp.bfloat16)
        payload = lax.optimization_barrier(payload).astype(jnp.float32)
        index = jnp.where(targets >= 0, (targets * SEGMENT_COUNT + segment_ids) * BLOCKS_DEV + target_blocks, drop_index)
        totals = totals.at[index.reshape(-1)].add(payload.reshape(-1, FEATURES, BLOCK_COLS), mode='drop')
        return (totals, None)
    totals = jnp.zeros((drop_index, FEATURES, BLOCK_COLS), jnp.float32)
    totals = lax.scan(band_step, totals, (grid_in, block_weights, dest_band, dest_block))[0]
    summed = totals.reshape(BAND_COUNT, SEGMENT_COUNT, BLOCKS_DEV, FEATURES, BLOCK_COLS)
    summed = summed.transpose(3, 0, 1, 2, 4).reshape(FIELDS, LEVELS, LATITUDES * LONGITUDES)
    below, diagonal, above = vertical_operator(lower_coef, upper_coef)
    solved = lax.linalg.tridiagonal_solve(below, diagonal, above, summed)
    grid_adj = solved.reshape(FIELDS, LEVELS, LATITUDES, LONGITUDES)
    table = fourier_table(order_pairs)
    fourier = jnp.dot(solved.reshape(FEATURES * LATITUDES, LONGITUDES).astype(jnp.float32), table.astype(jnp.float32), precision=lax.Precision.HIGHEST, preferred_element_type=jnp.float32).astype(jnp.bfloat16)
    fourier = lax.optimization_barrier(fourier).astype(jnp.float32)
    fourier = fourier.reshape(FEATURES, LATITUDES, PAIR_COUNT, 4).transpose(2, 0, 1, 3)
    degree_ids = jnp.arange(ORDERS + 1, dtype=jnp.int32)
    first_part = degree_ids[None, :] < (ORDERS - order_pairs)[:, None]

    def one_pair(slices):
        table_pair, fourier_pair, first_pair = slices
        mixed = jnp.einsum('nc,fnx->cxf', table_pair.astype(jnp.float32), fourier_pair)
        mixed = mixed.reshape(ORDERS + 1, 2, 2, FEATURES)
        return jnp.where(first_pair[:, None, None], mixed[:, 0], mixed[:, 1])
    spectral = lax.map(one_pair, (legendre, fourier, first_part))
    return (grid_adj, spectral)
```

```python
import math

import jax
import jax.numpy as jnp
from jax import lax
from jax.experimental import pallas as pl
from jax.experimental.pallas import tpu as pltpu
from jax.sharding import PartitionSpec as P

FIELDS = 4
LEVELS = 16
FEATURES = 64
LONGITUDES = 2560
ORDERS = 1280
LAT_DEV = 5
BANDS = 64
GROUPS = 4
CHIPS = 32
REACH = 5
CAP = 40
BLOCK = 128
PACK = CAP * FEATURES + 16
UNROLL = 10
SLOTS = 100
COL_BLOCKS = 20
LATITUDES = 1280
MIB = 1 << 20
F32 = jnp.float32
BF16 = jnp.bfloat16
VMEM = pl.BlockSpec(memory_space=pltpu.VMEM)
SMEM = pl.BlockSpec(memory_space=pltpu.SMEM)
HBM = pl.BlockSpec(memory_space=pl.ANY)


def iota(shape, dim):
    return lax.broadcasted_iota(jnp.int32, shape, dim)


def turned(steps):
    steps = steps - LONGITUDES * jnp.floor((steps + 0.5) * (1.0 / LONGITUDES))
    away = jnp.abs(steps - ORDERS)
    near = jnp.minimum(away, ORDERS - away)
    angle = near * (math.pi / ORDERS)
    t = angle * angle
    value = -1.0 / 87178291200.0
    for term in (479001600.0, -3628800.0, 40320.0, -720.0, 24.0, -2.0, 1.0):
        value = value * t + 1.0 / term
    return jnp.where(away > ORDERS // 2, value, -value)


def solve_rows(below, diagonal, above, start):
    ratios, values = [], []
    for k in range(LEVELS):
        if k == 0:
            inverse = 1.0 / diagonal[0]
            values.append(start[0] * inverse)
        else:
            inverse = 1.0 / (diagonal[k] - below[k] * ratios[k - 1])
            values.append((start[k] - below[k] * values[k - 1]) * inverse)
        ratios.append(above[k] * inverse if k < LEVELS - 1 else None)
    for k in range(LEVELS - 2, -1, -1):
        values[k] = values[k] - ratios[k] * values[k + 1]
    return values


def table_columns(orders, core):
    lane = iota((8, 2 * BLOCK), 1)
    within = lane & (BLOCK - 1)
    slot = (within & 31) * 2 + jnp.where(lane < BLOCK, core, 1 - core)
    order = jnp.zeros((8, 2 * BLOCK), jnp.int32)
    for p in range(BANDS):
        order = jnp.where(slot == p, orders[p], order)
    order = jnp.where((within & 32) == 0, order, ORDERS - 1 - order).astype(F32)
    quarter = jnp.where((within & 64) == 0, 0.0, float(LONGITUDES // 4))
    return order[0:1], quarter[0:1]


def write_table(order, quarter, table_ref):
    inner = iota((BLOCK, 2 * BLOCK), 0).astype(F32) * order
    cos_in = turned(inner)
    sin_in = turned(inner + 3.0 * (LONGITUDES // 4))
    scale = 1.0 / math.sqrt(LONGITUDES)
    outer = iota((24, 2 * BLOCK), 0).astype(F32) * (BLOCK * order) + quarter
    cos_out = turned(outer) * scale
    sin_out = turned(outer + 3.0 * (LONGITUDES // 4)) * scale
    for block in range(COL_BLOCKS):
        full = cos_out[block : block + 1] * cos_in - sin_out[block : block + 1] * sin_in
        head = full.astype(BF16)
        table_ref[block, 0:BLOCK, :] = head
        table_ref[block, BLOCK:, :] = (full - head.astype(F32)).astype(BF16)


def solve_kernel(lower_ref, upper_ref, lifts, lift_ref, work):
    lower, upper = lower_ref[...], upper_ref[...]
    lows = [jnp.broadcast_to(lower[:, k : k + 1], (FIELDS, BLOCK)) for k in range(LEVELS)]
    ups = [jnp.broadcast_to(upper[:, k : k + 1], (FIELDS, BLOCK)) for k in range(LEVELS)]
    diagonal = [1.0 + lows[k] + ups[k] for k in range(LEVELS)]
    col = iota((FIELDS, BLOCK), 1)
    mine = ((col >> 4) & 3) == iota((FIELDS, BLOCK), 0)
    zero = jnp.zeros((FIELDS, BLOCK), F32)
    unit = [jnp.where((col & 15) == k, 1.0, 0.0) for k in range(LEVELS)]
    shift_down = [zero] + [-ups[k - 1] for k in range(1, LEVELS)]
    shift_up = [-lows[k + 1] for k in range(LEVELS - 1)] + [zero]
    rows = solve_rows(shift_down, diagonal, shift_up, unit)
    for k in range(LEVELS):
        work[pl.ds(k, FIELDS, stride=LEVELS), :] = jnp.where(mine, rows[k], 0.0)
    full = work[...]
    head = full.astype(BF16).astype(F32)
    lift_ref[...] = jnp.where(iota((FEATURES, BLOCK), 1) < FEATURES, head, full - head).astype(BF16)
    plain_down = [zero] + [-lows[k] for k in range(1, LEVELS)]
    plain_up = [-ups[k] for k in range(LEVELS - 1)] + [zero]
    rows = solve_rows(plain_down, diagonal, plain_up, unit)
    for k in range(LEVELS):
        work[pl.ds(k, FIELDS, stride=LEVELS), :] = rows[k]
    wide = jnp.concatenate([work[...]] * FIELDS, axis=1)
    row = iota(wide.shape, 0)
    lane = iota(wide.shape, 1)
    owned = (row >> 4) == (lane >> 7)
    for q in range(8):
        full = jnp.where(owned & (((lane & 127) >> 4) == q), wide, 0.0)
        head = full.astype(BF16)
        lifts[q, 0:64] = head
        lifts[q, 64:128] = head
        lifts[q, 128:192] = (full - head.astype(F32)).astype(BF16)
        lifts[q, 192:256] = jnp.zeros_like(head)


def block_row(block):
    return (
        (block >= 20).astype(jnp.int32)
        + (block >= 40).astype(jnp.int32)
        + (block >= 60).astype(jnp.int32)
        + (block >= 80).astype(jnp.int32)
    )


def payload_kernel(
    dest_band, dest_block, orders, arrival_in, weights_in,
    own_part, other_part, kept, pair_out, near_out, up_out, down_out,
    arrival, weights, table, packs, tags, counts, places, in_sems, out_sems,
):
    band = lax.axis_index("band")
    core = lax.rem(band, 2)
    loads = [pltpu.make_async_copy(arrival_in, arrival, in_sems.at[LAT_DEV])]
    for lat in range(LAT_DEV):
        part = pl.ds(lat * COL_BLOCKS, COL_BLOCKS)
        loads.append(
            pltpu.make_async_copy(weights_in.at[part], weights.at[part], in_sems.at[lat])
        )
    for load in loads:
        load.start()
    for g in range(REACH):
        counts[g] = 0
    tags[...] = jnp.zeros_like(tags)
    own_part[...] = jnp.zeros_like(own_part)
    other_part[...] = jnp.zeros_like(other_part)
    write_table(*table_columns(orders, core), table)
    lane = iota((16, BLOCK), 1)

    def weigh(col, lat):
        j = lat * COL_BLOCKS + col
        rows = arrival[:, lat, :, pl.ds(pl.multiple_of(col * BLOCK, BLOCK), BLOCK)]
        payload = jnp.dot(
            rows.reshape(FEATURES, BLOCK), weights[j], preferred_element_type=F32
        ).astype(BF16)
        g = dest_band[j] - band + 2
        rank = counts[g]
        counts[g] = rank + 1
        start = pl.multiple_of(g * PACK + rank * FEATURES, 16)
        places[j] = start
        packs[pl.ds(start, FEATURES), :] = payload
        tag = (dest_block[j] + 1).astype(F32)
        tags[g] = jnp.where(lane == rank, tag, tags[g])
        return lat

    loads[0].wait()
    for lat in range(LAT_DEV):
        loads[1 + lat].wait()
        lax.fori_loop(0, COL_BLOCKS, weigh, lat, unroll=UNROLL)
    for g in range(REACH):
        packs[g * PACK + CAP * FEATURES : (g + 1) * PACK, :] = tags[g].astype(BF16)

    def ship(group, out, n):
        source = packs.at[pl.ds(pl.multiple_of(group * PACK, 16), PACK)]
        return pltpu.make_async_copy(source, out, out_sems.at[n])

    shipped = [
        ship(2, kept, 0),
        ship(3 - 2 * core, pair_out, 1),
        ship(1 + 2 * core, near_out, 2),
        ship(4, up_out, 3),
        ship(0, down_out, 4),
    ]
    for copy in shipped:
        copy.start()

    def analyse(j, carry):
        payload = packs[pl.ds(pl.multiple_of(places[j], 16), FEATURES), :]
        block = dest_block[j]
        lat = block_row(block)
        at = (dest_band[j] - band + 2) * LAT_DEV + lat
        col = block - lat * COL_BLOCKS
        twice = jnp.concatenate([payload, payload], axis=1)
        part = jnp.dot(twice, table[col], preferred_element_type=F32)
        own_part[at] = own_part[at] + part[:, :BLOCK]
        other_part[at] = other_part[at] + part[:, BLOCK:]
        return carry

    lax.fori_loop(0, SLOTS, analyse, 0, unroll=UNROLL)
    for copy in shipped:
        copy.wait()


def spread_kernel(own, other, lifts, out, turned_rows, work):
    core = lax.rem(lax.axis_index("band"), 2)
    for near in range(6):
        for i in range(LAT_DEV):
            if near == 0:
                total = jnp.where(core == 0, own[i], other[i])
            elif near == 5:
                total = jnp.where(core == 1, own[20 + i], other[20 + i])
            else:
                total = own[(near - core) * LAT_DEV + i] + other[(near - 1 + core) * LAT_DEV + i]
            head = total.astype(BF16).astype(F32)
            flipped = jnp.concatenate([head, total - head], axis=0).T.astype(BF16)
            at = (near // 2) * LAT_DEV + i
            for q in range(4):
                turned_rows[(near % 2) * 4 + q, at * 32 : (at + 1) * 32, :] = flipped[
                    q * 32 : (q + 1) * 32
                ]
    for chunk in range(5):
        total = jnp.zeros((96, 4 * BLOCK), F32)
        for q in range(8):
            part = turned_rows[q, chunk * 96 : (chunk + 1) * 96, :]
            total = total + jnp.dot(
                jnp.concatenate([part, part], axis=1), lifts[q], preferred_element_type=F32
            )
        for r in range(3):
            for g in range(GROUPS):
                work[pl.ds(g * 16 + chunk * 3 + r, 32, stride=64), :] = total[
                    r * 32 : (r + 1) * 32, g * BLOCK : (g + 1) * BLOCK
                ]
    for g in range(GROUPS):
        work[pl.ds(g * 16 + 15, 32, stride=64), :] = jnp.zeros((32, BLOCK), F32)
    out[...] = work[...].astype(BF16).reshape(out.shape)


def legendre_kernel(orders, parts, legendre, out, work, gathered):
    first = ORDERS - orders[lax.axis_index("band")]
    work[...] = parts[...].astype(F32).reshape(work.shape)
    for chip in range(CHIPS):
        for s in range(GROUPS):
            base = (chip * GROUPS + s) * 16
            total = work[base + 5 : base + 10, :]
            if chip > 0:
                total = total + work[base - 64 + 10 : base - 64 + 15, :]
            if chip < CHIPS - 1:
                total = total + work[base + 64 : base + 64 + 5, :]
            at = chip * 40 + s * LAT_DEV
            gathered[at : at + LAT_DEV, :] = total
            gathered[at + 20 : at + 20 + LAT_DEV, :] = pltpu.roll(total, 64, 1)
    right = gathered[...].astype(BF16)
    step = 256
    for low in range(0, ORDERS + 1, step):
        size = min(step, ORDERS + 1 - low)
        mixed = jnp.dot(legendre[low : low + size, :], right, preferred_element_type=F32).T
        degree = low + iota((16, size), 1)
        for r in range(2):
            picked = jnp.where(
                degree < first, mixed[r * 32 : r * 32 + 16], mixed[r * 32 + 16 : r * 32 + 32]
            )
            out[r, :, low : low + size] = picked


def grid_kernel(lift, *refs):
    sources = refs[:REACH]
    out, packs, work, tag_rows, tags, found, in_sems, tag_sem, out_sems = refs[REACH:]
    loads = [
        pltpu.make_async_copy(
            source, packs.at[pl.ds(n * PACK, PACK)], in_sems.at[n]
        )
        for n, source in enumerate(sources)
    ]
    for load in loads:
        load.start()
    for load in loads:
        load.wait()
    for n in range(REACH):
        row = packs[n * PACK + CAP * FEATURES : (n + 1) * PACK, :]
        tag_rows[n : n + 1, :] = row.astype(F32)[0:1].astype(jnp.int32)
    copy = pltpu.make_async_copy(tag_rows, tags, tag_sem)
    copy.start()
    copy.wait()

    for n in range(REACH):

        def note(r, carry):
            found[tags[n, r]] = n * PACK + r * FEATURES
            return carry

        lax.fori_loop(0, CAP, note, 0, unroll=8)
    head = lift[...]
    copies = []
    for lat in range(LAT_DEV):
        for col in range(0, COL_BLOCKS, 2):
            tag = lat * COL_BLOCKS + col + 1
            rows = jnp.concatenate(
                [
                    packs[pl.ds(pl.multiple_of(found[tag + n], 16), FEATURES), :]
                    for n in range(2)
                ],
                axis=1,
            )
            value = jnp.dot(
                head, jnp.concatenate([rows, rows], axis=0), preferred_element_type=F32
            )
            work[:, lat, :, col * BLOCK : (col + 2) * BLOCK] = value.reshape(
                FIELDS, LEVELS, 2 * BLOCK
            )
        copies.append(
            pltpu.make_async_copy(work.at[:, lat], out.at[:, lat], out_sems.at[lat])
        )
        copies[-1].start()
    for copy in copies:
        copy.wait()


def call(kernel, ins, outs, shapes, scratch, name, flops, limit=16):
    return pl.pallas_call(
        kernel,
        in_specs=ins,
        out_specs=outs,
        out_shape=[jax.ShapeDtypeStruct(s, d) for s, d in shapes],
        scratch_shapes=scratch,
        name=name,
        cost_estimate=pl.CostEstimate(flops=flops, bytes_accessed=4 * MIB, transcendentals=0),
        compiler_params=pltpu.CompilerParams(vmem_limit_bytes=limit * MIB),
    )


def on_device(
    arrival_adj, block_weights, dest_band, dest_block, lower_coef, upper_coef, order_pairs, legendre
):
    arrival = arrival_adj.transpose(0, 2, 1, 3)
    weights = block_weights.reshape(SLOTS, BLOCK, BLOCK)
    targets = dest_band.reshape(SLOTS)
    blocks = dest_block.reshape(SLOTS)
    part_shape = ((REACH * LAT_DEV, FEATURES, BLOCK), F32)
    pack_shape = ((PACK, BLOCK), BF16)
    own, other, kept, pair, near, up, down = call(
        payload_kernel,
        [SMEM, SMEM, SMEM, HBM, HBM],
        [VMEM, VMEM] + [HBM] * 5,
        [part_shape] * 2 + [pack_shape] * 5,
        [
            pltpu.VMEM((FIELDS, LAT_DEV, LEVELS, LONGITUDES), BF16),
            pltpu.VMEM((SLOTS, BLOCK, BLOCK), BF16),
            pltpu.VMEM((COL_BLOCKS, 2 * BLOCK, 2 * BLOCK), BF16),
            pltpu.VMEM((REACH * PACK, BLOCK), BF16),
            pltpu.VMEM((REACH, 16, BLOCK), F32),
            pltpu.SMEM((8,), jnp.int32),
            pltpu.SMEM((SLOTS,), jnp.int32),
            pltpu.SemaphoreType.DMA((LAT_DEV + 1,)),
            pltpu.SemaphoreType.DMA((5,)),
        ],
        "payload_and_part_fourier",
        3 * 10**9,
        56,
    )(targets, blocks, order_pairs, arrival, weights)
    lifts, lift = call(
        solve_kernel,
        [VMEM, VMEM],
        [VMEM] * 2,
        [((8, 2 * BLOCK, 4 * BLOCK), BF16), ((FEATURES, BLOCK), BF16)],
        [pltpu.VMEM((FEATURES, BLOCK), F32)],
        "inverse_of_vertical_operator",
        10**9,
    )(lower_coef, upper_coef)

    swap = [(b, b ^ 1) for b in range(BANDS)]
    hop = [(b, b + 1) for b in range(1, BANDS - 1, 2)] + [(b, b - 1) for b in range(2, BANDS, 2)]
    rise = [(b, b + 2) for b in range(BANDS - 2)]
    fall = [(b, b - 2) for b in range(2, BANDS)]
    other = lax.ppermute(other, "band", swap)
    (message,) = call(
        spread_kernel,
        [VMEM] * 3,
        [VMEM],
        [((CHIPS * GROUPS, 16, BLOCK), BF16)],
        [
            pltpu.VMEM((8, 480, BLOCK), BF16),
            pltpu.VMEM((CHIPS * GROUPS * 16, BLOCK), F32),
        ],
        "vertical_solve_of_fourier",
        10**9,
    )(own, other, lifts)
    same_core = [
        [(chip * 2 + core) * GROUPS + s for chip in range(CHIPS) for s in range(GROUPS)]
        for core in range(2)
    ]
    parts = lax.all_to_all(
        message, ("band", "lev"), split_axis=0, concat_axis=0, axis_index_groups=same_core, tiled=True
    )
    received = [
        kept,
        lax.ppermute(pair, "band", swap),
        lax.ppermute(near, "band", hop),
        lax.ppermute(up, "band", rise),
        lax.ppermute(down, "band", fall),
    ]
    (grid_adj,) = call(
        grid_kernel,
        [VMEM] + [HBM] * REACH,
        [HBM],
        [((FIELDS, LAT_DEV, LEVELS, LONGITUDES), F32)],
        [
            pltpu.VMEM((REACH * PACK, BLOCK), BF16),
            pltpu.VMEM((FIELDS, LAT_DEV, LEVELS, LONGITUDES), F32),
            pltpu.VMEM((8, BLOCK), jnp.int32),
            pltpu.SMEM((8, BLOCK), jnp.int32),
            pltpu.SMEM((SLOTS + 1,), jnp.int32),
            pltpu.SemaphoreType.DMA((REACH,)),
            pltpu.SemaphoreType.DMA,
            pltpu.SemaphoreType.DMA((LAT_DEV,)),
        ],
        "grid_vertical_solve",
        2 * 10**9,
    )(lift, *received)
    (spectral,) = call(
        legendre_kernel,
        [SMEM, VMEM, VMEM],
        [VMEM],
        [((2, LEVELS, ORDERS + 1), F32)],
        [
            pltpu.VMEM((CHIPS * GROUPS * 16, BLOCK), F32),
            pltpu.VMEM((LATITUDES, BLOCK), F32),
        ],
        "legendre_analysis",
        2 * 10**9,
    )(order_pairs, parts, legendre[0].T)
    return (grid_adj.transpose(0, 2, 1, 3), spectral.transpose(2, 0, 1)[None])


def solution(mesh):
    in_specs = (
        P(None, None, ("band", "lev"), None),
        P("band", "lev", None, None, None),
        P("band", "lev", None),
        P("band", "lev", None),
        P(),
        P(),
        P(),
        P("band", None, None),
    )
    out_specs = (P(None, None, ("band", "lev"), None), P("band", None, None, "lev"))
    return jax.shard_map(
        on_device, mesh=mesh, in_specs=in_specs, out_specs=out_specs, check_vma=False
    )
```

```python
import functools
import math

import jax
import jax.numpy as jnp
from jax import lax
from jax.experimental import pallas as pl
from jax.experimental.pallas import tpu as pltpu
from jax.sharding import PartitionSpec as P

FIELDS = 4
LEVELS = 16
FEATURES = 64
LONGITUDES = 2560
ORDERS = 1280
LAT_DEV = 5
BANDS = 64
GROUPS = 4
CHIPS = 32
REACH = 5
CAP = 40
FAR = 20
BLOCK = 128
TAG_ROWS = 16
PACK = TAG_ROWS + CAP * FEATURES
UNROLL = 10
SLOTS = 100
COL_BLOCKS = 20
LATITUDES = 1280
MIB = 1 << 20
F32 = jnp.float32
BF16 = jnp.bfloat16
VMEM = pl.BlockSpec(memory_space=pltpu.VMEM)
SMEM = pl.BlockSpec(memory_space=pltpu.SMEM)
HBM = pl.BlockSpec(memory_space=pltpu.HBM)
ANY = pl.BlockSpec(memory_space=pl.ANY)


def iota(shape, dim):
    return lax.broadcasted_iota(jnp.int32, shape, dim)


def turned(steps):
    steps = steps - LONGITUDES * jnp.floor((steps + 0.5) * (1.0 / LONGITUDES))
    away = jnp.abs(steps - ORDERS)
    near = jnp.minimum(away, ORDERS - away)
    angle = near * (math.pi / ORDERS)
    t = angle * angle
    value = -1.0 / 87178291200.0
    for term in (479001600.0, -3628800.0, 40320.0, -720.0, 24.0, -2.0, 1.0):
        value = value * t + 1.0 / term
    return jnp.where(away > ORDERS // 2, value, -value)


def solve_rows(below, diagonal, above, start):
    ratios, values = [], []
    for k in range(LEVELS):
        if k == 0:
            inverse = 1.0 / diagonal[0]
            values.append(start[0] * inverse)
        else:
            inverse = 1.0 / (diagonal[k] - below[k] * ratios[k - 1])
            values.append((start[k] - below[k] * values[k - 1]) * inverse)
        ratios.append(above[k] * inverse if k < LEVELS - 1 else None)
    for k in range(LEVELS - 2, -1, -1):
        values[k] = values[k] - ratios[k] * values[k + 1]
    return values


def write_tables(orders, core, inner_table, angles):
    lane = iota((8, BLOCK), 1)
    slot = (lane & 31) * 2 + jnp.where(lane < 64, core, 1 - core)
    order = jnp.zeros((8, BLOCK), jnp.int32)
    for p in range(BANDS):
        order = jnp.where(slot == p, orders[p], order)
    order = jnp.where((lane & 32) == 0, order, ORDERS - 1 - order).astype(F32)[0:1]
    three_quarters = 3.0 * (LONGITUDES // 4)
    inner = iota((BLOCK, BLOCK), 0).astype(F32) * order
    for part, full in enumerate((turned(inner), turned(inner + three_quarters))):
        head = full.astype(BF16)
        cols = slice(part * BLOCK, (part + 1) * BLOCK)
        inner_table[0:BLOCK, cols] = head
        inner_table[BLOCK:, cols] = (full - head.astype(F32)).astype(BF16)
    scale = 1.0 / math.sqrt(LONGITUDES)
    outer = iota((24, BLOCK), 0).astype(F32) * (BLOCK * order)
    angles[0] = turned(outer) * scale
    angles[1] = turned(outer + three_quarters) * scale


def solve_kernel(lower_in, upper_in, sums, lifts, lift_ref, own_part, lower_ref, upper_ref, work, sems):
    loads = [
        pltpu.make_async_copy(lower_in, lower_ref, sems.at[0]),
        pltpu.make_async_copy(upper_in, upper_ref, sems.at[1]),
    ]
    for load in loads:
        load.start()
    half = iota((FEATURES, BLOCK), 1) < 64

    def split(at, carry):
        real = sums[at, :, :BLOCK]
        imaginary = sums[at, :, BLOCK:]
        own_part[at] = jnp.where(half, real, pltpu.roll(imaginary, 64, 1))
        return carry

    lax.fori_loop(0, REACH * LAT_DEV + 1, split, 0, unroll=13)
    for load in loads:
        load.wait()
    lower, upper = lower_ref[...], upper_ref[...]
    lows = [jnp.broadcast_to(lower[:, k : k + 1], (FIELDS, BLOCK)) for k in range(LEVELS)]
    ups = [jnp.broadcast_to(upper[:, k : k + 1], (FIELDS, BLOCK)) for k in range(LEVELS)]
    diagonal = [1.0 + lows[k] + ups[k] for k in range(LEVELS)]
    col = iota((FIELDS, BLOCK), 1)
    mine = ((col >> 4) & 3) == iota((FIELDS, BLOCK), 0)
    zero = jnp.zeros((FIELDS, BLOCK), F32)
    unit = [jnp.where((col & 15) == k, 1.0, 0.0) for k in range(LEVELS)]
    shift_down = [zero] + [-ups[k - 1] for k in range(1, LEVELS)]
    shift_up = [-lows[k + 1] for k in range(LEVELS - 1)] + [zero]
    rows = solve_rows(shift_down, diagonal, shift_up, unit)
    for k in range(LEVELS):
        work[pl.ds(k, FIELDS, stride=LEVELS), :] = jnp.where(mine, rows[k], 0.0)
    full = work[...]
    head = full.astype(BF16).astype(F32)
    lift_ref[...] = jnp.where(iota((FEATURES, BLOCK), 1) < FEATURES, head, full - head).astype(BF16)
    plain_down = [zero] + [-lows[k] for k in range(1, LEVELS)]
    plain_up = [-ups[k] for k in range(LEVELS - 1)] + [zero]
    rows = solve_rows(plain_down, diagonal, plain_up, unit)
    for k in range(LEVELS):
        work[pl.ds(k, FIELDS, stride=LEVELS), :] = rows[k]
    wide = jnp.concatenate([work[...]] * FIELDS, axis=1)
    owned = (iota(wide.shape, 0) >> 4) == (iota(wide.shape, 1) >> 7)
    full = jnp.where(owned, wide, 0.0)
    head = full.astype(BF16)
    lifts[0:64] = head
    lifts[64:128] = head
    lifts[128:192] = (full - head.astype(F32)).astype(BF16)
    lifts[192:256] = jnp.zeros_like(head)


def block_row(block):
    return (
        (block >= 20).astype(jnp.int32)
        + (block >= 40).astype(jnp.int32)
        + (block >= 60).astype(jnp.int32)
        + (block >= 80).astype(jnp.int32)
    )


def pack_rows(cap):
    return TAG_ROWS + cap * FEATURES


def payload_kernel(
    far, dest_band_in, dest_block_in, orders_in, arrival_in, weights_in,
    sums, other_part, kept, pair_out, transit_out, hop_out,
    dest_band, dest_block, orders, arrival, weights, inner_table, angles, packs, tags, line, waves,
    counts, small_sems, in_sems, out_sems,
):
    band = lax.axis_index("band")
    core = lax.rem(band, 2)
    small = [
        pltpu.make_async_copy(source, held, small_sems.at[n])
        for n, (source, held) in enumerate(
            ((orders_in, orders), (dest_band_in, dest_band), (dest_block_in, dest_block))
        )
    ]
    for copy in small:
        copy.start()
    loads = []
    for lat in range(LAT_DEV):
        part = pl.ds(lat * COL_BLOCKS, COL_BLOCKS)
        loads.append(
            (
                pltpu.make_async_copy(arrival_in.at[:, lat], arrival.at[:, lat], in_sems.at[2 * lat]),
                pltpu.make_async_copy(weights_in.at[part], weights.at[part], in_sems.at[2 * lat + 1]),
            )
        )
        for load in loads[-1]:
            load.start()
    far_rows = pack_rows(far)
    for g in range(REACH):
        counts[g] = 0
    tags[...] = jnp.zeros_like(tags)
    sums[...] = jnp.zeros_like(sums)
    for copy in small:
        copy.wait()
    write_tables(orders, core, inner_table, angles)
    lane = iota((TAG_ROWS, BLOCK), 1)

    def weigh(col, lat):
        j = lat * COL_BLOCKS + col
        rows = arrival[:, lat, :, pl.ds(pl.multiple_of(col * BLOCK, BLOCK), BLOCK)]
        payload = jnp.dot(
            rows.reshape(FEATURES, BLOCK), weights[j], preferred_element_type=F32
        ).astype(BF16)
        line[pl.ds(pl.multiple_of(j * FEATURES, FEATURES), FEATURES), :] = payload
        g = dest_band[j] - band + 2
        rank = counts[g]
        counts[g] = rank + 1
        start = pl.multiple_of(g * PACK + TAG_ROWS + rank * FEATURES, 16)
        packs[pl.ds(start, FEATURES), :] = payload
        tag = (dest_block[j] + 1).astype(F32)
        tags[g] = jnp.where(lane == rank, tag, tags[g])
        return lat

    for lat in range(LAT_DEV):
        for load in loads[lat]:
            load.wait()
        lax.fori_loop(0, COL_BLOCKS, weigh, lat, unroll=UNROLL)
    for g in range(REACH):
        packs[g * PACK : g * PACK + TAG_ROWS, :] = tags[g].astype(BF16)

    def ship(group, size, out, at, n):
        source = packs.at[pl.ds(pl.multiple_of(group * PACK, 16), size)]
        return pltpu.make_async_copy(source, out.at[pl.ds(at, size)], out_sems.at[n])

    shipped = [
        ship(4 - 4 * core, far_rows, transit_out, 0, 1),
        ship(1 + 2 * core, far_rows, hop_out, 0, 2),
        ship(4 * core, far_rows, hop_out, far_rows, 3),
        ship(3 - 2 * core, PACK, pair_out, 0, 0),
        ship(2, PACK, kept, 0, 4),
    ]
    for copy in shipped:
        copy.start()

    def transform(n, carry):
        rows = pl.ds(pl.multiple_of(n * 640, 640), 640)
        part = line[rows, :]
        waves[rows, :] = jnp.dot(
            jnp.concatenate([part, part], axis=1), inner_table[...], preferred_element_type=F32
        )
        return carry

    lax.fori_loop(0, 10, transform, 0)

    def analyse(j, carry):
        rows = pl.ds(pl.multiple_of(j * FEATURES, FEATURES), FEATURES)
        block = dest_block[j]
        lat = block_row(block)
        at = (dest_band[j] - band + 2) * LAT_DEV + lat
        col = block - lat * COL_BLOCKS
        cosine = angles[0, pl.ds(col, 1), :]
        sine = angles[1, pl.ds(col, 1), :]
        even = waves[rows, :BLOCK]
        odd = waves[rows, BLOCK:]
        sums[at, :, :BLOCK] = sums[at, :, :BLOCK] + (even * cosine - odd * sine)
        sums[at, :, BLOCK:] = sums[at, :, BLOCK:] - (even * sine + odd * cosine)
        return carry

    lax.fori_loop(0, SLOTS, analyse, 0, unroll=UNROLL)
    longest = jnp.maximum(
        jnp.maximum(counts[4 - 4 * core], counts[1 + 2 * core]), counts[4 * core]
    )
    overflow = jnp.where(longest > far, 1.0, 0.0)
    sums[REACH * LAT_DEV] = jnp.full((FEATURES, 2 * BLOCK), overflow, F32)
    half = iota((FEATURES, BLOCK), 1) < 64

    def split(at, carry):
        real = sums[at, :, :BLOCK]
        imaginary = sums[at, :, BLOCK:]
        other_part[at] = jnp.where(half, pltpu.roll(real, 64, 1), imaginary)
        return carry

    lax.fori_loop(0, REACH * LAT_DEV + 1, split, 0, unroll=13)
    for copy in shipped:
        copy.wait()


def spread_kernel(
    own, other, lifts, hop_own, transit, out, hop_out, turned_rows, work, carried, sems
):
    core = lax.rem(lax.axis_index("band"), 2)
    far_rows = transit.shape[0]
    fetch = pltpu.make_async_copy(transit, carried, sems.at[0])
    store = pltpu.make_async_copy(
        carried, hop_out.at[pl.ds(2 * far_rows, far_rows)], sems.at[1]
    )
    fetch.start()
    for near in range(6):
        for i in range(LAT_DEV):
            if near == 0:
                total = jnp.where(core == 0, own[i], other[i])
            elif near == 5:
                total = jnp.where(core == 1, own[20 + i], other[20 + i])
            else:
                total = own[(near - core) * LAT_DEV + i] + other[(near - 1 + core) * LAT_DEV + i]
            head = total.astype(BF16).astype(F32)
            flipped = jnp.concatenate([head, total - head], axis=0).T.astype(BF16)
            at = ((near // 2) * LAT_DEV + i) * 8 + (near % 2) * 4
            turned_rows[at * 32 : (at + 4) * 32, :] = flipped
    fetch.wait()
    store.start()
    group = (iota((32, 4 * BLOCK), 1) & (BLOCK - 1)) >> 4
    for chunk in range(5):
        part = turned_rows[chunk * 768 : (chunk + 1) * 768, :]
        raised = jnp.dot(
            jnp.concatenate([part, part], axis=1), lifts[...], preferred_element_type=F32
        )
        for r in range(3):
            total = raised[r * 256 : r * 256 + 32]
            for q in range(1, 8):
                low = r * 256 + q * 32
                total = jnp.where(group == q, raised[low : low + 32], total)
            for g in range(GROUPS):
                work[pl.ds(g * 16 + chunk * 3 + r, 32, stride=64), :] = total[
                    :, g * BLOCK : (g + 1) * BLOCK
                ]
    last = REACH * LAT_DEV
    overflow = jnp.maximum(own[last, 0:32, :], other[last, 0:32, :])
    for g in range(GROUPS):
        work[pl.ds(g * 16 + 15, 32, stride=64), :] = overflow
    out[...] = work[...].astype(BF16).reshape(out.shape)
    store.wait()


def legendre_kernel(
    orders_in, parts_in, legendre_in, grid_done, out, overflow,
    orders, parts, work, gathered, legendre, order_sem, part_sem, load_sem,
):
    fetch = pltpu.make_async_copy(orders_in, orders, order_sem)
    fetch.start()
    bring = pltpu.make_async_copy(parts_in, parts, part_sem)
    bring.start()
    load = pltpu.make_async_copy(legendre_in, legendre, load_sem)
    load.start()
    fetch.wait()
    first = ORDERS - orders[lax.axis_index("band")]
    bring.wait()
    work[...] = parts[...].astype(F32).reshape(work.shape)
    flags = work[pl.ds(15, CHIPS * GROUPS, stride=16), :]
    overflow[...] = jnp.broadcast_to(jnp.max(flags, axis=0, keepdims=True), overflow.shape)
    for chip in range(CHIPS):
        for s in range(GROUPS):
            base = (chip * GROUPS + s) * 16
            total = work[base + 5 : base + 10, :]
            if chip > 0:
                total = total + work[base - 64 + 10 : base - 64 + 15, :]
            if chip < CHIPS - 1:
                total = total + work[base + 64 : base + 64 + 5, :]
            at = chip * 40 + s * LAT_DEV
            gathered[at : at + LAT_DEV, :] = total
            gathered[at + 20 : at + 20 + LAT_DEV, :] = pltpu.roll(total, 64, 1)
    right = gathered[...].astype(BF16)
    load.wait()
    step = 256
    for low in range(0, ORDERS + 1, step):
        size = min(step, ORDERS + 1 - low)
        mixed = jnp.dot(legendre[low : low + size, :], right, preferred_element_type=F32).T
        degree = low + iota((16, size), 1)
        for r in range(2):
            picked = jnp.where(
                degree < first, mixed[r * 32 : r * 32 + 16], mixed[r * 32 + 16 : r * 32 + 32]
            )
            out[r, :, low : low + size] = picked


def grid_kernel(far, lift, kept, pair_in, hop_in, passed, *refs):
    out, done, packs, work, tag_rows, tags, found, in_sems, tag_sem, out_sems = refs
    far_rows = pack_rows(far)
    sources = [
        (kept, 0, PACK, CAP),
        (pair_in, 0, PACK, CAP),
        (hop_in, 0, far_rows, far),
        (hop_in, 2 * far_rows, far_rows, far),
        (passed, 0, far_rows, far),
    ]
    starts = [0, PACK, 2 * PACK, 2 * PACK + far_rows, 2 * PACK + 2 * far_rows]
    loads = [
        pltpu.make_async_copy(
            source.at[pl.ds(low, size)], packs.at[pl.ds(starts[n], size)], in_sems.at[n]
        )
        for n, (source, low, size, _) in enumerate(sources)
    ]
    for load in loads:
        load.start()
    for load in loads:
        load.wait()
    for n in range(REACH):
        row = packs[starts[n] : starts[n] + TAG_ROWS, :]
        tag_rows[n : n + 1, :] = row.astype(F32)[0:1].astype(jnp.int32)
    copy = pltpu.make_async_copy(tag_rows, tags, tag_sem)
    copy.start()
    copy.wait()

    def clear(n, carry):
        found[n] = TAG_ROWS
        return carry

    lax.fori_loop(0, SLOTS + 1, clear, 0)
    for n in range(REACH):

        def note(r, carry):
            found[tags[n, r]] = starts[n] + TAG_ROWS + r * FEATURES
            return carry

        lax.fori_loop(0, sources[n][3], note, 0, unroll=10)
    head = lift[...]
    copies = []
    for lat in range(LAT_DEV):
        for col in range(0, COL_BLOCKS, 2):
            tag = lat * COL_BLOCKS + col + 1
            rows = jnp.concatenate(
                [
                    packs[pl.ds(pl.multiple_of(found[tag + n], 16), FEATURES), :]
                    for n in range(2)
                ],
                axis=1,
            )
            value = jnp.dot(
                head, jnp.concatenate([rows, rows], axis=0), preferred_element_type=F32
            )
            work[:, lat, :, col * BLOCK : (col + 2) * BLOCK] = value.reshape(
                FIELDS, LEVELS, 2 * BLOCK
            )
        copies.append(
            pltpu.make_async_copy(work.at[:, lat], out.at[:, lat], out_sems.at[lat])
        )
        copies[-1].start()
    done[...] = jnp.zeros_like(done)
    for copy in copies:
        copy.wait()


def call(kernel, ins, outs, shapes, scratch, name, flops, limit=22, aliases={}):
    return pl.pallas_call(
        kernel,
        in_specs=ins,
        out_specs=outs,
        out_shape=[jax.ShapeDtypeStruct(s, d) for s, d in shapes],
        scratch_shapes=scratch,
        name=name,
        input_output_aliases=aliases,
        cost_estimate=pl.CostEstimate(flops=flops, bytes_accessed=4 * MIB, transcendentals=0),
        compiler_params=pltpu.CompilerParams(vmem_limit_bytes=limit * MIB),
    )


def payloads(far, targets, blocks, order_pairs, arrival, weights):
    part_count = REACH * LAT_DEV + 1
    return call(
        functools.partial(payload_kernel, far),
        [HBM] * 5,
        [VMEM, VMEM] + [HBM] * 4,
        [((part_count, FEATURES, 2 * BLOCK), F32), ((part_count, FEATURES, BLOCK), F32)]
        + [((rows, BLOCK), BF16) for rows in (PACK, PACK, pack_rows(far), 3 * pack_rows(far))],
        [
            pltpu.SMEM((SLOTS,), jnp.int32),
            pltpu.SMEM((SLOTS,), jnp.int32),
            pltpu.SMEM((BANDS,), jnp.int32),
            pltpu.VMEM((FIELDS, LAT_DEV, LEVELS, LONGITUDES), BF16),
            pltpu.VMEM((SLOTS, BLOCK, BLOCK), BF16),
            pltpu.VMEM((2 * BLOCK, 2 * BLOCK), BF16),
            pltpu.VMEM((2, 24, BLOCK), F32),
            pltpu.VMEM((REACH * PACK, BLOCK), BF16),
            pltpu.VMEM((REACH, TAG_ROWS, BLOCK), F32),
            pltpu.VMEM((SLOTS * FEATURES, BLOCK), BF16),
            pltpu.VMEM((SLOTS * FEATURES, 2 * BLOCK), F32),
            pltpu.SMEM((8,), jnp.int32),
            pltpu.SemaphoreType.DMA((3,)),
            pltpu.SemaphoreType.DMA((2 * LAT_DEV,)),
            pltpu.SemaphoreType.DMA((5,)),
        ],
        "payload_and_part_fourier",
        3 * 10**9,
        36,
    )(targets, blocks, order_pairs, arrival, weights)


def grid_solve(far, lift, kept, pair, hop_all, passed):
    return call(
        functools.partial(grid_kernel, far),
        [VMEM] + [ANY] * 4,
        [HBM, VMEM],
        [((FIELDS, LAT_DEV, LEVELS, LONGITUDES), F32), ((8, BLOCK), F32)],
        [
            pltpu.VMEM((2 * PACK + 3 * pack_rows(far), BLOCK), BF16),
            pltpu.VMEM((FIELDS, LAT_DEV, LEVELS, LONGITUDES), F32),
            pltpu.VMEM((8, BLOCK), jnp.int32),
            pltpu.SMEM((8, BLOCK), jnp.int32),
            pltpu.SMEM((SLOTS + 1,), jnp.int32),
            pltpu.SemaphoreType.DMA((REACH,)),
            pltpu.SemaphoreType.DMA,
            pltpu.SemaphoreType.DMA((LAT_DEV,)),
        ],
        "grid_vertical_solve",
        2 * 10**9,
    )(lift, kept, pair, hop_all, passed)


SWAP = [(b, b ^ 1) for b in range(BANDS)]
HOP = [(b, b + 1) for b in range(1, BANDS - 1, 2)] + [(b, b - 1) for b in range(2, BANDS, 2)]


def on_device(
    arrival_adj, block_weights, dest_band, dest_block, lower_coef, upper_coef, order_pairs, legendre
):
    arrival = arrival_adj.transpose(0, 2, 1, 3)
    weights = block_weights.reshape(SLOTS, BLOCK, BLOCK)
    targets = dest_band.reshape(SLOTS)
    blocks = dest_block.reshape(SLOTS)
    sums, other, kept, pair, transit, hop_own = payloads(
        FAR, targets, blocks, order_pairs, arrival, weights
    )
    other = lax.ppermute(other, "band", SWAP)
    transit = lax.ppermute(transit, "band", SWAP)
    lifts, lift, own = call(
        solve_kernel,
        [HBM, HBM, VMEM],
        [VMEM] * 3,
        [
            ((2 * BLOCK, 4 * BLOCK), BF16),
            ((FEATURES, BLOCK), BF16),
            ((REACH * LAT_DEV + 1, FEATURES, BLOCK), F32),
        ],
        [
            pltpu.VMEM((FIELDS, LEVELS), F32),
            pltpu.VMEM((FIELDS, LEVELS), F32),
            pltpu.VMEM((FEATURES, BLOCK), F32),
            pltpu.SemaphoreType.DMA((2,)),
        ],
        "inverse_of_vertical_operator",
        10**9,
    )(lower_coef, upper_coef, sums)
    message, hop_all = call(
        spread_kernel,
        [VMEM] * 3 + [HBM, ANY],
        [VMEM, HBM],
        [((CHIPS * GROUPS, 16, BLOCK), BF16), ((3 * pack_rows(FAR), BLOCK), BF16)],
        [
            pltpu.VMEM((3840, BLOCK), BF16),
            pltpu.VMEM((CHIPS * GROUPS * 16, BLOCK), F32),
            pltpu.VMEM((pack_rows(FAR), BLOCK), BF16),
            pltpu.SemaphoreType.DMA((2,)),
        ],
        "vertical_solve_of_fourier",
        10**9,
        aliases={3: 1},
    )(own, other, lifts, hop_own, transit)
    message, hop_all, pair = lax.optimization_barrier((message, hop_all, pair))
    hop_all = lax.ppermute(hop_all, "band", HOP)
    pair = lax.ppermute(pair, "band", SWAP)
    same_core = [
        [(chip * 2 + core) * GROUPS + s for chip in range(CHIPS) for s in range(GROUPS)]
        for core in range(2)
    ]
    parts = lax.all_to_all(
        message, ("band", "lev"), split_axis=0, concat_axis=0, axis_index_groups=same_core, tiled=True
    )
    passed = lax.ppermute(hop_all[pack_rows(FAR) : 2 * pack_rows(FAR)], "band", SWAP)
    grid_adj, grid_done = grid_solve(FAR, lift, kept, pair, hop_all, passed)
    spectral, overflow = call(
        legendre_kernel,
        [HBM, ANY, HBM, ANY],
        [VMEM] * 2,
        [((2, LEVELS, ORDERS + 1), F32), ((8, BLOCK), F32)],
        [
            pltpu.SMEM((BANDS,), jnp.int32),
            pltpu.VMEM((CHIPS * GROUPS, 16, BLOCK), BF16),
            pltpu.VMEM((CHIPS * GROUPS * 16, BLOCK), F32),
            pltpu.VMEM((LATITUDES, BLOCK), F32),
            pltpu.VMEM((ORDERS + 1, LATITUDES), BF16),
            pltpu.SemaphoreType.DMA,
            pltpu.SemaphoreType.DMA,
            pltpu.SemaphoreType.DMA,
        ],
        "legendre_analysis",
        2 * 10**9,
        56,
    )(order_pairs, parts, legendre[0].T, grid_done)

    def wide_exchange(state):
        _, kept, pair, transit, hop = payloads(
            CAP, targets, blocks, order_pairs, arrival, weights
        )[1:]
        pair = lax.ppermute(pair, "band", SWAP)
        transit = lax.ppermute(transit, "band", SWAP)
        hop = lax.ppermute(jnp.concatenate([hop[: 2 * PACK], transit]), "band", HOP)
        passed = lax.ppermute(hop[PACK : 2 * PACK], "band", SWAP)
        return (jnp.float32(0.0), grid_solve(CAP, lift, kept, pair, hop, passed)[0])

    _, grid_adj = lax.while_loop(
        lambda state: state[0] > 0.0, wide_exchange, (overflow[0, 0], grid_adj)
    )
    return (grid_adj.transpose(0, 2, 1, 3), spectral.transpose(2, 0, 1)[None])


def solution(mesh):
    in_specs = (
        P(None, None, ("band", "lev"), None),
        P("band", "lev", None, None, None),
        P("band", "lev", None),
        P("band", "lev", None),
        P(),
        P(),
        P(),
        P("band", None, None),
    )
    out_specs = (P(None, None, ("band", "lev"), None), P("band", None, None, "lev"))
    return jax.shard_map(
        on_device, mesh=mesh, in_specs=in_specs, out_specs=out_specs, check_vma=False
    )
```

```python
import functools
import math

import jax
import jax.numpy as jnp
from jax import lax
from jax.experimental import pallas as pl
from jax.experimental.pallas import tpu as pltpu
from jax.sharding import PartitionSpec as P

FIELDS = 4
LEVELS = 16
FEATURES = 64
LONGITUDES = 2560
ORDERS = 1280
LAT_DEV = 5
BANDS = 64
GROUPS = 4
CHIPS = 32
REACH = 5
CAP = 40
FAR = 20
BLOCK = 128
TAG_ROWS = 16
PACK = TAG_ROWS + CAP * FEATURES
UNROLL = 20
AHEAD = 2
SLOTS = 100
COL_BLOCKS = 20
LATITUDES = 1280
MIB = 1 << 20
F32 = jnp.float32
BF16 = jnp.bfloat16
VMEM = pl.BlockSpec(memory_space=pltpu.VMEM)
SMEM = pl.BlockSpec(memory_space=pltpu.SMEM)
HBM = pl.BlockSpec(memory_space=pltpu.HBM)
ANY = pl.BlockSpec(memory_space=pl.ANY)


def iota(shape, dim):
    return lax.broadcasted_iota(jnp.int32, shape, dim)


def turned(steps):
    steps = steps - LONGITUDES * jnp.floor((steps + 0.5) * (1.0 / LONGITUDES))
    away = jnp.abs(steps - ORDERS)
    near = jnp.minimum(away, ORDERS - away)
    angle = near * (math.pi / ORDERS)
    t = angle * angle
    value = -1.0 / 87178291200.0
    for term in (479001600.0, -3628800.0, 40320.0, -720.0, 24.0, -2.0, 1.0):
        value = value * t + 1.0 / term
    return jnp.where(away > ORDERS // 2, value, -value)


def solve_rows(below, diagonal, above, start):
    ratios, values = [], []
    for k in range(LEVELS):
        if k == 0:
            inverse = 1.0 / diagonal[0]
            values.append(start[0] * inverse)
        else:
            inverse = 1.0 / (diagonal[k] - below[k] * ratios[k - 1])
            values.append((start[k] - below[k] * values[k - 1]) * inverse)
        ratios.append(above[k] * inverse if k < LEVELS - 1 else None)
    for k in range(LEVELS - 2, -1, -1):
        values[k] = values[k] - ratios[k] * values[k + 1]
    return values


def write_tables(orders, core, inner_table, angles):
    lane = iota((8, BLOCK), 1)
    slot = (lane & 31) * 2 + jnp.where(lane < 64, core, 1 - core)
    order = jnp.zeros((8, BLOCK), jnp.int32)
    for p in range(BANDS):
        order = jnp.where(slot == p, orders[p], order)
    order = jnp.where((lane & 32) == 0, order, ORDERS - 1 - order).astype(F32)[0:1]
    three_quarters = 3.0 * (LONGITUDES // 4)
    inner = iota((BLOCK, BLOCK), 0).astype(F32) * order
    for part, full in enumerate((turned(inner), turned(inner + three_quarters))):
        head = full.astype(BF16)
        cols = slice(part * BLOCK, (part + 1) * BLOCK)
        inner_table[0:BLOCK, cols] = head
        inner_table[BLOCK:, cols] = (full - head.astype(F32)).astype(BF16)
    scale = 1.0 / math.sqrt(LONGITUDES)
    outer = iota((24, BLOCK), 0).astype(F32) * (BLOCK * order)
    angles[0] = turned(outer) * scale
    angles[1] = turned(outer + three_quarters) * scale


def solve_kernel(lower_in, upper_in, sums, lifts, lift_ref, own_part, lower_ref, upper_ref, work, sems):
    loads = [
        pltpu.make_async_copy(lower_in, lower_ref, sems.at[0]),
        pltpu.make_async_copy(upper_in, upper_ref, sems.at[1]),
    ]
    for load in loads:
        load.start()
    half = iota((FEATURES, BLOCK), 1) < 64

    def split(at, carry):
        real = sums[at, :, :BLOCK]
        imaginary = sums[at, :, BLOCK:]
        own_part[at] = jnp.where(half, real, pltpu.roll(imaginary, 64, 1))
        return carry

    lax.fori_loop(0, REACH * LAT_DEV + 1, split, 0, unroll=13)
    for load in loads:
        load.wait()
    lower, upper = lower_ref[...], upper_ref[...]
    lows = [jnp.broadcast_to(lower[:, k : k + 1], (FIELDS, BLOCK)) for k in range(LEVELS)]
    ups = [jnp.broadcast_to(upper[:, k : k + 1], (FIELDS, BLOCK)) for k in range(LEVELS)]
    diagonal = [1.0 + lows[k] + ups[k] for k in range(LEVELS)]
    col = iota((FIELDS, BLOCK), 1)
    mine = ((col >> 4) & 3) == iota((FIELDS, BLOCK), 0)
    zero = jnp.zeros((FIELDS, BLOCK), F32)
    unit = [jnp.where((col & 15) == k, 1.0, 0.0) for k in range(LEVELS)]
    shift_down = [zero] + [-ups[k - 1] for k in range(1, LEVELS)]
    shift_up = [-lows[k + 1] for k in range(LEVELS - 1)] + [zero]
    rows = solve_rows(shift_down, diagonal, shift_up, unit)
    for k in range(LEVELS):
        work[pl.ds(k, FIELDS, stride=LEVELS), :] = jnp.where(mine, rows[k], 0.0)
    full = work[...]
    head = full.astype(BF16).astype(F32)
    lift_ref[...] = jnp.where(iota((FEATURES, BLOCK), 1) < FEATURES, head, full - head).astype(BF16)
    plain_down = [zero] + [-lows[k] for k in range(1, LEVELS)]
    plain_up = [-ups[k] for k in range(LEVELS - 1)] + [zero]
    rows = solve_rows(plain_down, diagonal, plain_up, unit)
    for k in range(LEVELS):
        work[pl.ds(k, FIELDS, stride=LEVELS), :] = rows[k]
    wide = jnp.concatenate([work[...]] * FIELDS, axis=1)
    owned = (iota(wide.shape, 0) >> 4) == (iota(wide.shape, 1) >> 7)
    full = jnp.where(owned, wide, 0.0)
    head = full.astype(BF16)
    lifts[0:64] = head
    lifts[64:128] = head
    lifts[128:192] = (full - head.astype(F32)).astype(BF16)
    lifts[192:256] = jnp.zeros_like(head)


def block_row(block):
    return (
        (block >= 20).astype(jnp.int32)
        + (block >= 40).astype(jnp.int32)
        + (block >= 60).astype(jnp.int32)
        + (block >= 80).astype(jnp.int32)
    )


def pack_rows(cap):
    return TAG_ROWS + cap * FEATURES


def payload_kernel(
    far, dest_band_in, dest_block_in, orders_in, arrival_in, weights_in,
    sums, other_part, kept, pair_out, transit_out, hop_out,
    dest_band, dest_block, orders, arrival, weights, inner_table, angles, packs, tags, line, waves,
    counts, small_sems, in_sems, out_sems,
):
    band = lax.axis_index("band")
    core = lax.rem(band, 2)
    small = [
        pltpu.make_async_copy(source, held, small_sems.at[n])
        for n, (source, held) in enumerate(
            ((orders_in, orders), (dest_band_in, dest_band), (dest_block_in, dest_block))
        )
    ]
    for copy in small:
        copy.start()
    loads = []
    for lat in range(LAT_DEV):
        part = pl.ds(lat * COL_BLOCKS, COL_BLOCKS)
        loads.append(
            (
                pltpu.make_async_copy(arrival_in.at[:, lat], arrival.at[:, lat], in_sems.at[2 * lat]),
                pltpu.make_async_copy(weights_in.at[part], weights.at[part], in_sems.at[2 * lat + 1]),
            )
        )
    for ahead in range(AHEAD):
        for load in loads[ahead]:
            load.start()
    far_rows = pack_rows(far)
    for g in range(REACH):
        counts[g] = 0
    tags[...] = jnp.zeros_like(tags)
    sums[...] = jnp.zeros_like(sums)
    for copy in small:
        copy.wait()
    write_tables(orders, core, inner_table, angles)
    lane = iota((TAG_ROWS, BLOCK), 1)

    def weigh(col, lat):
        j = lat * COL_BLOCKS + col
        rows = arrival[:, lat, :, pl.ds(pl.multiple_of(col * BLOCK, BLOCK), BLOCK)]
        payload = jnp.dot(
            rows.reshape(FEATURES, BLOCK), weights[j], preferred_element_type=F32
        ).astype(BF16)
        line[pl.ds(pl.multiple_of(j * FEATURES, FEATURES), FEATURES), :] = jnp.concatenate(
            [payload, payload], axis=1
        )
        g = dest_band[j] - band + 2
        rank = counts[g]
        counts[g] = rank + 1
        start = pl.multiple_of(g * PACK + TAG_ROWS + rank * FEATURES, 16)
        packs[pl.ds(start, FEATURES), :] = payload
        tag = (dest_block[j] + 1).astype(F32)
        tags[g] = jnp.where(lane == rank, tag, tags[g])
        return lat

    def ship(group, size, out, at, n):
        source = packs.at[pl.ds(pl.multiple_of(group * PACK, 16), size)]
        return pltpu.make_async_copy(source, out.at[pl.ds(at, size)], out_sems.at[n])

    shipped = [
        ship(4 - 4 * core, far_rows, transit_out, 0, 1),
        ship(1 + 2 * core, far_rows, hop_out, 0, 2),
        ship(4 * core, far_rows, hop_out, far_rows, 3),
        ship(3 - 2 * core, PACK, pair_out, 0, 0),
        ship(2, PACK, kept, 0, 4),
    ]

    def transform(lat):
        rows = pl.ds(lat * COL_BLOCKS * FEATURES, COL_BLOCKS * FEATURES)
        waves[rows, :] = jnp.dot(line[rows, :], inner_table[...], preferred_element_type=F32)

    def analyse(j, carry):
        rows = pl.ds(pl.multiple_of(j * FEATURES, FEATURES), FEATURES)
        block = dest_block[j]
        lat = block_row(block)
        at = (dest_band[j] - band + 2) * LAT_DEV + lat
        col = block - lat * COL_BLOCKS
        cosine = angles[0, pl.ds(col, 1), :]
        sine = angles[1, pl.ds(col, 1), :]
        even = waves[rows, :BLOCK]
        odd = waves[rows, BLOCK:]
        sums[at, :, :BLOCK] = sums[at, :, :BLOCK] + (even * cosine - odd * sine)
        sums[at, :, BLOCK:] = sums[at, :, BLOCK:] - (even * sine + odd * cosine)
        return carry

    for lat in range(LAT_DEV):
        for load in loads[lat]:
            load.wait()
        if lat + AHEAD < LAT_DEV:
            for load in loads[lat + AHEAD]:
                load.start()
        lax.fori_loop(0, COL_BLOCKS, weigh, lat, unroll=UNROLL)
        if lat == LAT_DEV - 1:
            for g in range(REACH):
                packs[g * PACK : g * PACK + TAG_ROWS, :] = tags[g].astype(BF16)
            for copy in shipped:
                copy.start()
        transform(lat)
        lax.fori_loop(COL_BLOCKS * lat, COL_BLOCKS * (lat + 1), analyse, 0, unroll=UNROLL)
    longest = jnp.maximum(
        jnp.maximum(counts[4 - 4 * core], counts[1 + 2 * core]), counts[4 * core]
    )
    overflow = jnp.where(longest > far, 1.0, 0.0)
    sums[REACH * LAT_DEV] = jnp.full((FEATURES, 2 * BLOCK), overflow, F32)
    half = iota((FEATURES, BLOCK), 1) < 64

    def split(at, carry):
        real = sums[at, :, :BLOCK]
        imaginary = sums[at, :, BLOCK:]
        other_part[at] = jnp.where(half, pltpu.roll(real, 64, 1), imaginary)
        return carry

    lax.fori_loop(0, REACH * LAT_DEV + 1, split, 0, unroll=13)
    for copy in shipped:
        copy.wait()


def spread_kernel(
    own, other, lifts, hop_own, transit, out, hop_out, turned_rows, work, carried, sems
):
    core = lax.rem(lax.axis_index("band"), 2)
    far_rows = transit.shape[0]
    fetch = pltpu.make_async_copy(transit, carried, sems.at[0])
    store = pltpu.make_async_copy(
        carried, hop_out.at[pl.ds(2 * far_rows, far_rows)], sems.at[1]
    )
    fetch.start()
    for near in range(6):
        for i in range(LAT_DEV):
            if near == 0:
                total = jnp.where(core == 0, own[i], other[i])
            elif near == 5:
                total = jnp.where(core == 1, own[20 + i], other[20 + i])
            else:
                total = own[(near - core) * LAT_DEV + i] + other[(near - 1 + core) * LAT_DEV + i]
            head = total.astype(BF16).astype(F32)
            flipped = jnp.concatenate([head, total - head], axis=0).T.astype(BF16)
            at = ((near // 2) * LAT_DEV + i) * 8 + (near % 2) * 4
            turned_rows[at * 32 : (at + 4) * 32, :] = flipped
    fetch.wait()
    store.start()
    group = (iota((32, 4 * BLOCK), 1) & (BLOCK - 1)) >> 4
    for chunk in range(5):
        part = turned_rows[chunk * 768 : (chunk + 1) * 768, :]
        raised = jnp.dot(
            jnp.concatenate([part, part], axis=1), lifts[...], preferred_element_type=F32
        )
        for r in range(3):
            total = raised[r * 256 : r * 256 + 32]
            for q in range(1, 8):
                low = r * 256 + q * 32
                total = jnp.where(group == q, raised[low : low + 32], total)
            for g in range(GROUPS):
                work[pl.ds(g * 16 + chunk * 3 + r, 32, stride=64), :] = total[
                    :, g * BLOCK : (g + 1) * BLOCK
                ]
    last = REACH * LAT_DEV
    overflow = jnp.maximum(own[last, 0:32, :], other[last, 0:32, :])
    for g in range(GROUPS):
        work[pl.ds(g * 16 + 15, 32, stride=64), :] = overflow
    out[...] = work[...].astype(BF16).reshape(out.shape)
    store.wait()


def legendre_kernel(
    orders_in, parts_in, legendre_in, grid_done, out, overflow,
    orders, parts, work, gathered, legendre, order_sem, part_sem, load_sem,
):
    fetch = pltpu.make_async_copy(orders_in, orders, order_sem)
    fetch.start()
    bring = pltpu.make_async_copy(parts_in, parts, part_sem)
    bring.start()
    load = pltpu.make_async_copy(legendre_in, legendre, load_sem)
    load.start()
    fetch.wait()
    first = ORDERS - orders[lax.axis_index("band")]
    bring.wait()
    work[...] = parts[...].astype(F32).reshape(work.shape)
    flags = work[pl.ds(15, CHIPS * GROUPS, stride=16), :]
    overflow[0, 0] = jnp.max(flags)
    for chip in range(CHIPS):
        for s in range(GROUPS):
            base = (chip * GROUPS + s) * 16
            total = work[base + 5 : base + 10, :]
            if chip > 0:
                total = total + work[base - 64 + 10 : base - 64 + 15, :]
            if chip < CHIPS - 1:
                total = total + work[base + 64 : base + 64 + 5, :]
            at = chip * 40 + s * LAT_DEV
            gathered[at : at + LAT_DEV, :] = total
            gathered[at + 20 : at + 20 + LAT_DEV, :] = pltpu.roll(total, 64, 1)
    right = gathered[...].astype(BF16)
    load.wait()
    step = 256
    for low in range(0, ORDERS + 1, step):
        size = min(step, ORDERS + 1 - low)
        mixed = jnp.dot(legendre[low : low + size, :], right, preferred_element_type=F32).T
        degree = low + iota((16, size), 1)
        for r in range(2):
            picked = jnp.where(
                degree < first, mixed[r * 32 : r * 32 + 16], mixed[r * 32 + 16 : r * 32 + 32]
            )
            out[r, :, low : low + size] = picked


def grid_kernel(far, lift, kept, pair_in, hop_in, passed, *refs):
    out, done, packs, work, tag_rows, tags, found, in_sems, tag_sem, out_sems = refs
    far_rows = pack_rows(far)
    sources = [
        (kept, 0, PACK, CAP),
        (pair_in, 0, PACK, CAP),
        (hop_in, 0, far_rows, far),
        (hop_in, 2 * far_rows, far_rows, far),
        (passed, 0, far_rows, far),
    ]
    starts = [0, PACK, 2 * PACK, 2 * PACK + far_rows, 2 * PACK + 2 * far_rows]
    loads = [
        pltpu.make_async_copy(
            source.at[pl.ds(low, size)], packs.at[pl.ds(starts[n], size)], in_sems.at[n]
        )
        for n, (source, low, size, _) in enumerate(sources)
    ]
    for load in loads:
        load.start()
    for load in loads:
        load.wait()
    for n in range(REACH):
        row = packs[starts[n] : starts[n] + TAG_ROWS, :]
        tag_rows[n : n + 1, :] = row.astype(F32)[0:1].astype(jnp.int32)
    copy = pltpu.make_async_copy(tag_rows, tags, tag_sem)
    copy.start()
    copy.wait()

    def clear(n, carry):
        found[n] = TAG_ROWS
        return carry

    lax.fori_loop(0, SLOTS + 1, clear, 0)
    for n in range(REACH):

        def note(r, carry):
            found[tags[n, r]] = starts[n] + TAG_ROWS + r * FEATURES
            return carry

        lax.fori_loop(0, sources[n][3], note, 0, unroll=10)
    head = lift[...]
    copies = []
    for lat in range(LAT_DEV):
        for col in range(0, COL_BLOCKS, 2):
            tag = lat * COL_BLOCKS + col + 1
            rows = jnp.concatenate(
                [
                    packs[pl.ds(pl.multiple_of(found[tag + n], 16), FEATURES), :]
                    for n in range(2)
                ],
                axis=1,
            )
            value = jnp.dot(
                head, jnp.concatenate([rows, rows], axis=0), preferred_element_type=F32
            )
            work[:, lat, :, col * BLOCK : (col + 2) * BLOCK] = value.reshape(
                FIELDS, LEVELS, 2 * BLOCK
            )
        copies.append(
            pltpu.make_async_copy(work.at[:, lat], out.at[:, lat], out_sems.at[lat])
        )
        copies[-1].start()
    done[...] = jnp.zeros_like(done)
    for copy in copies:
        copy.wait()


def call(kernel, ins, outs, shapes, scratch, name, flops, limit=22, aliases={}):
    return pl.pallas_call(
        kernel,
        in_specs=ins,
        out_specs=outs,
        out_shape=[jax.ShapeDtypeStruct(s, d) for s, d in shapes],
        scratch_shapes=scratch,
        name=name,
        input_output_aliases=aliases,
        cost_estimate=pl.CostEstimate(flops=flops, bytes_accessed=4 * MIB, transcendentals=0),
        compiler_params=pltpu.CompilerParams(vmem_limit_bytes=limit * MIB),
    )


def payloads(far, targets, blocks, order_pairs, arrival, weights):
    part_count = REACH * LAT_DEV + 1
    return call(
        functools.partial(payload_kernel, far),
        [HBM] * 5,
        [VMEM, VMEM] + [HBM] * 4,
        [((part_count, FEATURES, 2 * BLOCK), F32), ((part_count, FEATURES, BLOCK), F32)]
        + [((rows, BLOCK), BF16) for rows in (PACK, PACK, pack_rows(far), 3 * pack_rows(far))],
        [
            pltpu.SMEM((SLOTS,), jnp.int32),
            pltpu.SMEM((SLOTS,), jnp.int32),
            pltpu.SMEM((BANDS,), jnp.int32),
            pltpu.VMEM((FIELDS, LAT_DEV, LEVELS, LONGITUDES), BF16),
            pltpu.VMEM((SLOTS, BLOCK, BLOCK), BF16),
            pltpu.VMEM((2 * BLOCK, 2 * BLOCK), BF16),
            pltpu.VMEM((2, 24, BLOCK), F32),
            pltpu.VMEM((REACH * PACK, BLOCK), BF16),
            pltpu.VMEM((REACH, TAG_ROWS, BLOCK), F32),
            pltpu.VMEM((SLOTS * FEATURES, 2 * BLOCK), BF16),
            pltpu.VMEM((SLOTS * FEATURES, 2 * BLOCK), F32),
            pltpu.SMEM((8,), jnp.int32),
            pltpu.SemaphoreType.DMA((3,)),
            pltpu.SemaphoreType.DMA((2 * LAT_DEV,)),
            pltpu.SemaphoreType.DMA((5,)),
        ],
        "payload_and_part_fourier",
        3 * 10**9,
        36,
    )(targets, blocks, order_pairs, arrival, weights)


def grid_solve(far, lift, kept, pair, hop_all, passed):
    return call(
        functools.partial(grid_kernel, far),
        [VMEM] + [ANY] * 4,
        [HBM, VMEM],
        [((FIELDS, LAT_DEV, LEVELS, LONGITUDES), F32), ((8, BLOCK), F32)],
        [
            pltpu.VMEM((2 * PACK + 3 * pack_rows(far), BLOCK), BF16),
            pltpu.VMEM((FIELDS, LAT_DEV, LEVELS, LONGITUDES), F32),
            pltpu.VMEM((8, BLOCK), jnp.int32),
            pltpu.SMEM((8, BLOCK), jnp.int32),
            pltpu.SMEM((SLOTS + 1,), jnp.int32),
            pltpu.SemaphoreType.DMA((REACH,)),
            pltpu.SemaphoreType.DMA,
            pltpu.SemaphoreType.DMA((LAT_DEV,)),
        ],
        "grid_vertical_solve",
        2 * 10**9,
    )(lift, kept, pair, hop_all, passed)


SWAP = [(b, b ^ 1) for b in range(BANDS)]
HOP = [(b, b + 1) for b in range(1, BANDS - 1, 2)] + [(b, b - 1) for b in range(2, BANDS, 2)]


def on_device(
    arrival_adj, block_weights, dest_band, dest_block, lower_coef, upper_coef, order_pairs, legendre
):
    arrival = arrival_adj.transpose(0, 2, 1, 3)
    weights = block_weights.reshape(SLOTS, BLOCK, BLOCK)
    targets = dest_band.reshape(SLOTS)
    blocks = dest_block.reshape(SLOTS)
    sums, other, kept, pair, transit, hop_own = payloads(
        FAR, targets, blocks, order_pairs, arrival, weights
    )
    other = lax.ppermute(other, "band", SWAP)
    transit = lax.ppermute(transit, "band", SWAP)
    lifts, lift, own = call(
        solve_kernel,
        [HBM, HBM, VMEM],
        [VMEM] * 3,
        [
            ((2 * BLOCK, 4 * BLOCK), BF16),
            ((FEATURES, BLOCK), BF16),
            ((REACH * LAT_DEV + 1, FEATURES, BLOCK), F32),
        ],
        [
            pltpu.VMEM((FIELDS, LEVELS), F32),
            pltpu.VMEM((FIELDS, LEVELS), F32),
            pltpu.VMEM((FEATURES, BLOCK), F32),
            pltpu.SemaphoreType.DMA((2,)),
        ],
        "inverse_of_vertical_operator",
        10**9,
    )(lower_coef, upper_coef, sums)
    message, hop_all = call(
        spread_kernel,
        [VMEM] * 3 + [HBM, ANY],
        [VMEM, HBM],
        [((CHIPS * GROUPS, 16, BLOCK), BF16), ((3 * pack_rows(FAR), BLOCK), BF16)],
        [
            pltpu.VMEM((3840, BLOCK), BF16),
            pltpu.VMEM((CHIPS * GROUPS * 16, BLOCK), F32),
            pltpu.VMEM((pack_rows(FAR), BLOCK), BF16),
            pltpu.SemaphoreType.DMA((2,)),
        ],
        "vertical_solve_of_fourier",
        10**9,
        aliases={3: 1},
    )(own, other, lifts, hop_own, transit)
    message, hop_all, pair = lax.optimization_barrier((message, hop_all, pair))
    hop_all = lax.ppermute(hop_all, "band", HOP)
    pair = lax.ppermute(pair, "band", SWAP)
    same_core = [
        [(chip * 2 + core) * GROUPS + s for chip in range(CHIPS) for s in range(GROUPS)]
        for core in range(2)
    ]
    parts = lax.all_to_all(
        message, ("band", "lev"), split_axis=0, concat_axis=0, axis_index_groups=same_core, tiled=True
    )
    passed = lax.ppermute(hop_all[pack_rows(FAR) : 2 * pack_rows(FAR)], "band", SWAP)
    grid_adj, grid_done = grid_solve(FAR, lift, kept, pair, hop_all, passed)
    spectral, overflow = call(
        legendre_kernel,
        [HBM, ANY, HBM, ANY],
        [VMEM, SMEM],
        [((2, LEVELS, ORDERS + 1), F32), ((1, 1), F32)],
        [
            pltpu.SMEM((BANDS,), jnp.int32),
            pltpu.VMEM((CHIPS * GROUPS, 16, BLOCK), BF16),
            pltpu.VMEM((CHIPS * GROUPS * 16, BLOCK), F32),
            pltpu.VMEM((LATITUDES, BLOCK), F32),
            pltpu.VMEM((ORDERS + 1, LATITUDES), BF16),
            pltpu.SemaphoreType.DMA,
            pltpu.SemaphoreType.DMA,
            pltpu.SemaphoreType.DMA,
        ],
        "legendre_analysis",
        2 * 10**9,
        56,
    )(order_pairs, parts, legendre[0].T, grid_done)

    def wide_exchange(state):
        _, kept, pair, transit, hop = payloads(
            CAP, targets, blocks, order_pairs, arrival, weights
        )[1:]
        pair = lax.ppermute(pair, "band", SWAP)
        transit = lax.ppermute(transit, "band", SWAP)
        hop = lax.ppermute(jnp.concatenate([hop[: 2 * PACK], transit]), "band", HOP)
        passed = lax.ppermute(hop[PACK : 2 * PACK], "band", SWAP)
        return (jnp.float32(0.0), grid_solve(CAP, lift, kept, pair, hop, passed)[0])

    _, grid_adj = lax.while_loop(
        lambda state: state[0] > 0.0, wide_exchange, (overflow[0, 0], grid_adj)
    )
    return (grid_adj.transpose(0, 2, 1, 3), spectral.transpose(2, 0, 1)[None])


def solution(mesh):
    in_specs = (
        P(None, None, ("band", "lev"), None),
        P("band", "lev", None, None, None),
        P("band", "lev", None),
        P("band", "lev", None),
        P(),
        P(),
        P(),
        P("band", None, None),
    )
    out_specs = (P(None, None, ("band", "lev"), None), P("band", None, None, "lev"))
    return jax.shard_map(
        on_device, mesh=mesh, in_specs=in_specs, out_specs=out_specs, check_vma=False
    )
```

```python
import functools
import math

import jax
import jax.numpy as jnp
from jax import lax
from jax.experimental import pallas as pl
from jax.experimental.pallas import tpu as pltpu
from jax.sharding import PartitionSpec as P

FIELDS = 4
LEVELS = 16
FEATURES = 64
LONGITUDES = 2560
ORDERS = 1280
LAT_DEV = 5
BANDS = 64
GROUPS = 4
CHIPS = 32
REACH = 5
CAP = 40
FAR = 20
BLOCK = 128
TAG_ROWS = 16
PACK = TAG_ROWS + CAP * FEATURES
UNROLL = 20
AHEAD = 2
SLOTS = 100
COL_BLOCKS = 20
LATITUDES = 1280
MIB = 1 << 20
F32 = jnp.float32
BF16 = jnp.bfloat16
VMEM = pl.BlockSpec(memory_space=pltpu.VMEM)
SMEM = pl.BlockSpec(memory_space=pltpu.SMEM)
HBM = pl.BlockSpec(memory_space=pltpu.HBM)
ANY = pl.BlockSpec(memory_space=pl.ANY)


def iota(shape, dim):
    return lax.broadcasted_iota(jnp.int32, shape, dim)


def turned(steps):
    steps = steps - LONGITUDES * jnp.floor((steps + 0.5) * (1.0 / LONGITUDES))
    away = jnp.abs(steps - ORDERS)
    near = jnp.minimum(away, ORDERS - away)
    angle = near * (math.pi / ORDERS)
    t = angle * angle
    value = -1.0 / 87178291200.0
    for term in (479001600.0, -3628800.0, 40320.0, -720.0, 24.0, -2.0, 1.0):
        value = value * t + 1.0 / term
    return jnp.where(away > ORDERS // 2, value, -value)


def solve_rows(below, diagonal, above, start):
    ratios, values = [], []
    for k in range(LEVELS):
        if k == 0:
            inverse = 1.0 / diagonal[0]
            values.append(start[0] * inverse)
        else:
            inverse = 1.0 / (diagonal[k] - below[k] * ratios[k - 1])
            values.append((start[k] - below[k] * values[k - 1]) * inverse)
        ratios.append(above[k] * inverse if k < LEVELS - 1 else None)
    for k in range(LEVELS - 2, -1, -1):
        values[k] = values[k] - ratios[k] * values[k + 1]
    return values


def write_tables(orders, core, inner_table, angles):
    lane = iota((8, BLOCK), 1)
    slot = (lane & 31) * 2 + jnp.where(lane < 64, core, 1 - core)
    order = jnp.zeros((8, BLOCK), jnp.int32)
    for p in range(BANDS):
        order = jnp.where(slot == p, orders[p], order)
    order = jnp.where((lane & 32) == 0, order, ORDERS - 1 - order).astype(F32)[0:1]
    three_quarters = 3.0 * (LONGITUDES // 4)
    inner = iota((BLOCK, BLOCK), 0).astype(F32) * order
    for part, full in enumerate((turned(inner), turned(inner + three_quarters))):
        head = full.astype(BF16)
        cols = slice(part * BLOCK, (part + 1) * BLOCK)
        inner_table[0:BLOCK, cols] = head
        inner_table[BLOCK:, cols] = (full - head.astype(F32)).astype(BF16)
    scale = 1.0 / math.sqrt(LONGITUDES)
    outer = iota((24, BLOCK), 0).astype(F32) * (BLOCK * order)
    angles[0] = turned(outer) * scale
    angles[1] = turned(outer + three_quarters) * scale


def solve_kernel(lower_in, upper_in, sums, lifts, lift_ref, own_part, lower_ref, upper_ref, work, sems):
    loads = [
        pltpu.make_async_copy(lower_in, lower_ref, sems.at[0]),
        pltpu.make_async_copy(upper_in, upper_ref, sems.at[1]),
    ]
    for load in loads:
        load.start()
    half = iota((FEATURES, BLOCK), 1) < 64

    def split(at, carry):
        real = sums[at, :, :BLOCK]
        imaginary = sums[at, :, BLOCK:]
        own_part[at] = jnp.where(half, real, pltpu.roll(imaginary, 64, 1))
        return carry

    lax.fori_loop(0, REACH * LAT_DEV + 1, split, 0, unroll=13)
    for load in loads:
        load.wait()
    lower, upper = lower_ref[...], upper_ref[...]
    lows = [jnp.broadcast_to(lower[:, k : k + 1], (FIELDS, BLOCK)) for k in range(LEVELS)]
    ups = [jnp.broadcast_to(upper[:, k : k + 1], (FIELDS, BLOCK)) for k in range(LEVELS)]
    diagonal = [1.0 + lows[k] + ups[k] for k in range(LEVELS)]
    col = iota((FIELDS, BLOCK), 1)
    mine = ((col >> 4) & 3) == iota((FIELDS, BLOCK), 0)
    zero = jnp.zeros((FIELDS, BLOCK), F32)
    unit = [jnp.where((col & 15) == k, 1.0, 0.0) for k in range(LEVELS)]
    shift_down = [zero] + [-ups[k - 1] for k in range(1, LEVELS)]
    shift_up = [-lows[k + 1] for k in range(LEVELS - 1)] + [zero]
    rows = solve_rows(shift_down, diagonal, shift_up, unit)
    for k in range(LEVELS):
        work[pl.ds(k, FIELDS, stride=LEVELS), :] = jnp.where(mine, rows[k], 0.0)
    full = work[...]
    head = full.astype(BF16).astype(F32)
    lift_ref[...] = jnp.where(iota((FEATURES, BLOCK), 1) < FEATURES, head, full - head).astype(BF16)
    plain_down = [zero] + [-lows[k] for k in range(1, LEVELS)]
    plain_up = [-ups[k] for k in range(LEVELS - 1)] + [zero]
    rows = solve_rows(plain_down, diagonal, plain_up, unit)
    for k in range(LEVELS):
        work[pl.ds(k, FIELDS, stride=LEVELS), :] = rows[k]
    wide = jnp.concatenate([work[...]] * FIELDS, axis=1)
    owned = (iota(wide.shape, 0) >> 4) == (iota(wide.shape, 1) >> 7)
    full = jnp.where(owned, wide, 0.0)
    head = full.astype(BF16)
    lifts[0:64] = head
    lifts[64:128] = head
    lifts[128:192] = (full - head.astype(F32)).astype(BF16)
    lifts[192:256] = jnp.zeros_like(head)


def block_row(block):
    return (
        (block >= 20).astype(jnp.int32)
        + (block >= 40).astype(jnp.int32)
        + (block >= 60).astype(jnp.int32)
        + (block >= 80).astype(jnp.int32)
    )


def pack_rows(cap):
    return TAG_ROWS + cap * FEATURES


def payload_kernel(
    far, dest_band_in, dest_block_in, orders_in, arrival_in, weights_in,
    sums, other_part, kept, pair_out, transit_out, hop_out,
    dest_band, dest_block, orders, arrival, weights, inner_table, angles, packs, tags, line, waves,
    counts, small_sems, in_sems, out_sems,
):
    band = lax.axis_index("band")
    core = lax.rem(band, 2)
    small = [
        pltpu.make_async_copy(source, held, small_sems.at[n])
        for n, (source, held) in enumerate(
            ((orders_in, orders), (dest_band_in, dest_band), (dest_block_in, dest_block))
        )
    ]
    for copy in small:
        copy.start()
    loads = []
    for lat in range(LAT_DEV):
        part = pl.ds(lat * COL_BLOCKS, COL_BLOCKS)
        loads.append(
            (
                pltpu.make_async_copy(arrival_in.at[:, lat], arrival.at[:, lat], in_sems.at[2 * lat]),
                pltpu.make_async_copy(weights_in.at[part], weights.at[part], in_sems.at[2 * lat + 1]),
            )
        )
    for ahead in range(AHEAD):
        for load in loads[ahead]:
            load.start()
    far_rows = pack_rows(far)
    for g in range(REACH):
        counts[g] = 0
    tags[...] = jnp.zeros_like(tags)
    sums[...] = jnp.zeros_like(sums)
    for copy in small:
        copy.wait()
    write_tables(orders, core, inner_table, angles)
    lane = iota((TAG_ROWS, BLOCK), 1)

    def weigh(col, lat):
        j = lat * COL_BLOCKS + col
        rows = arrival[:, lat, :, pl.ds(pl.multiple_of(col * BLOCK, BLOCK), BLOCK)]
        payload = jnp.dot(
            rows.reshape(FEATURES, BLOCK), weights[j], preferred_element_type=F32
        ).astype(BF16)
        line[pl.ds(pl.multiple_of(j * FEATURES, FEATURES), FEATURES), :] = jnp.concatenate(
            [payload, payload], axis=1
        )
        g = dest_band[j] - band + 2
        rank = counts[g]
        counts[g] = rank + 1
        start = pl.multiple_of(g * PACK + TAG_ROWS + rank * FEATURES, 16)
        packs[pl.ds(start, FEATURES), :] = payload
        tag = (dest_block[j] + 1).astype(F32)
        tags[g] = jnp.where(lane == rank, tag, tags[g])
        return lat

    def ship(group, size, out, at, n):
        source = packs.at[pl.ds(pl.multiple_of(group * PACK, 16), size)]
        return pltpu.make_async_copy(source, out.at[pl.ds(at, size)], out_sems.at[n])

    shipped = [
        ship(4 - 4 * core, far_rows, transit_out, 0, 1),
        ship(1 + 2 * core, far_rows, hop_out, 0, 2),
        ship(4 * core, far_rows, hop_out, far_rows, 3),
        ship(3 - 2 * core, PACK, pair_out, 0, 0),
        ship(2, PACK, kept, 0, 4),
    ]

    def transform(lat):
        rows = pl.ds(lat * COL_BLOCKS * FEATURES, COL_BLOCKS * FEATURES)
        waves[rows, :] = jnp.dot(line[rows, :], inner_table[...], preferred_element_type=F32)

    def analyse(j, carry):
        rows = pl.ds(pl.multiple_of(j * FEATURES, FEATURES), FEATURES)
        block = dest_block[j]
        lat = block_row(block)
        at = (dest_band[j] - band + 2) * LAT_DEV + lat
        col = block - lat * COL_BLOCKS
        cosine = angles[0, pl.ds(col, 1), :]
        sine = angles[1, pl.ds(col, 1), :]
        even = waves[rows, :BLOCK]
        odd = waves[rows, BLOCK:]
        sums[at, :, :BLOCK] = sums[at, :, :BLOCK] + (even * cosine - odd * sine)
        sums[at, :, BLOCK:] = sums[at, :, BLOCK:] - (even * sine + odd * cosine)
        return carry

    for lat in range(LAT_DEV):
        for load in loads[lat]:
            load.wait()
        if lat + AHEAD < LAT_DEV:
            for load in loads[lat + AHEAD]:
                load.start()
        lax.fori_loop(0, COL_BLOCKS, weigh, lat, unroll=UNROLL)
        if lat == LAT_DEV - 1:
            for g in range(REACH):
                packs[g * PACK : g * PACK + TAG_ROWS, :] = tags[g].astype(BF16)
            for copy in shipped:
                copy.start()
        transform(lat)
        lax.fori_loop(COL_BLOCKS * lat, COL_BLOCKS * (lat + 1), analyse, 0, unroll=UNROLL)
    longest = jnp.maximum(
        jnp.maximum(counts[4 - 4 * core], counts[1 + 2 * core]), counts[4 * core]
    )
    overflow = jnp.where(longest > far, 1.0, 0.0)
    sums[REACH * LAT_DEV] = jnp.full((FEATURES, 2 * BLOCK), overflow, F32)
    half = iota((FEATURES, BLOCK), 1) < 64

    def split(at, carry):
        real = sums[at, :, :BLOCK]
        imaginary = sums[at, :, BLOCK:]
        other_part[at] = jnp.where(half, pltpu.roll(real, 64, 1), imaginary)
        return carry

    lax.fori_loop(0, REACH * LAT_DEV + 1, split, 0, unroll=13)
    for copy in shipped:
        copy.wait()


def spread_kernel(
    own, other, lifts, hop_own, transit, out, hop_out, turned_rows, work, sem
):
    core = lax.rem(lax.axis_index("band"), 2)
    far_rows = transit.shape[0]
    carry = pltpu.make_async_copy(
        transit, hop_out.at[pl.ds(2 * far_rows, far_rows)], sem
    )
    carry.start()
    for near in range(6):
        for i in range(LAT_DEV):
            if near == 0:
                total = jnp.where(core == 0, own[i], other[i])
            elif near == 5:
                total = jnp.where(core == 1, own[20 + i], other[20 + i])
            else:
                total = own[(near - core) * LAT_DEV + i] + other[(near - 1 + core) * LAT_DEV + i]
            head = total.astype(BF16).astype(F32)
            flipped = jnp.concatenate([head, total - head], axis=0).T.astype(BF16)
            at = ((near // 2) * LAT_DEV + i) * 8 + (near % 2) * 4
            turned_rows[at * 32 : (at + 4) * 32, :] = flipped
    group = (iota((32, 4 * BLOCK), 1) & (BLOCK - 1)) >> 4
    for chunk in range(5):
        part = turned_rows[chunk * 768 : (chunk + 1) * 768, :]
        raised = jnp.dot(
            jnp.concatenate([part, part], axis=1), lifts[...], preferred_element_type=F32
        )
        for r in range(3):
            total = raised[r * 256 : r * 256 + 32]
            for q in range(1, 8):
                low = r * 256 + q * 32
                total = jnp.where(group == q, raised[low : low + 32], total)
            for g in range(GROUPS):
                work[pl.ds(g * 16 + chunk * 3 + r, 32, stride=64), :] = total[
                    :, g * BLOCK : (g + 1) * BLOCK
                ]
    last = REACH * LAT_DEV
    overflow = jnp.maximum(own[last, 0:32, :], other[last, 0:32, :])
    for g in range(GROUPS):
        work[pl.ds(g * 16 + 15, 32, stride=64), :] = overflow
    out[...] = work[...].astype(BF16).reshape(out.shape)
    carry.wait()


def legendre_kernel(
    orders_in, parts_in, legendre_in, last_in, grid_done, out, overflow,
    orders, parts, work, gathered, legendre, last, order_sem, part_sem, load_sems,
):
    fetch = pltpu.make_async_copy(orders_in, orders, order_sem)
    fetch.start()
    bring = pltpu.make_async_copy(parts_in, parts, part_sem)
    bring.start()
    step = 256
    lows = list(range(0, ORDERS, step))
    loads = [
        pltpu.make_async_copy(
            legendre_in.at[pl.ds(low, step)], legendre.at[pl.ds(low, step)], load_sems.at[n]
        )
        for n, low in enumerate(lows)
    ]
    loads.append(pltpu.make_async_copy(last_in, last, load_sems.at[len(lows)]))
    for load in loads:
        load.start()
    fetch.wait()
    first = ORDERS - orders[lax.axis_index("band")]
    bring.wait()
    work[...] = parts[...].astype(F32).reshape(work.shape)
    flags = work[pl.ds(15, CHIPS * GROUPS, stride=16), :]
    overflow[0, 0] = jnp.max(flags)
    for chip in range(CHIPS):
        for s in range(GROUPS):
            base = (chip * GROUPS + s) * 16
            total = work[base + 5 : base + 10, :]
            if chip > 0:
                total = total + work[base - 64 + 10 : base - 64 + 15, :]
            if chip < CHIPS - 1:
                total = total + work[base + 64 : base + 64 + 5, :]
            at = chip * 40 + s * LAT_DEV
            gathered[at : at + LAT_DEV, :] = total
            gathered[at + 20 : at + 20 + LAT_DEV, :] = pltpu.roll(total, 64, 1)
    right = gathered[...].astype(BF16)
    for load, low in zip(loads, lows + [ORDERS]):
        load.wait()
        size = step if low < ORDERS else 1
        rows = legendre[low : low + size, :] if low < ORDERS else last[...]
        mixed = jnp.dot(rows, right, preferred_element_type=F32).T
        degree = low + iota((16, size), 1)
        for r in range(2):
            picked = jnp.where(
                degree < first, mixed[r * 32 : r * 32 + 16], mixed[r * 32 + 16 : r * 32 + 32]
            )
            out[r, :, low : low + size] = picked


def grid_kernel(far, lift, kept, pair_in, hop_in, passed, *refs):
    out, done, packs, work, tag_rows, tags, found, in_sems, tag_sem, out_sems = refs
    far_rows = pack_rows(far)
    sources = [
        (kept, 0, PACK, CAP),
        (pair_in, 0, PACK, CAP),
        (hop_in, 0, far_rows, far),
        (hop_in, 2 * far_rows, far_rows, far),
        (passed, 0, far_rows, far),
    ]
    starts = [0, PACK, 2 * PACK, 2 * PACK + far_rows, 2 * PACK + 2 * far_rows]
    loads = [
        pltpu.make_async_copy(
            source.at[pl.ds(low, size)], packs.at[pl.ds(starts[n], size)], in_sems.at[n]
        )
        for n, (source, low, size, _) in enumerate(sources)
    ]
    for load in loads:
        load.start()
    for load in loads:
        load.wait()
    for n in range(REACH):
        row = packs[starts[n] : starts[n] + TAG_ROWS, :]
        tag_rows[n : n + 1, :] = row.astype(F32)[0:1].astype(jnp.int32)
    copy = pltpu.make_async_copy(tag_rows, tags, tag_sem)
    copy.start()
    copy.wait()

    def clear(n, carry):
        found[n] = TAG_ROWS
        return carry

    lax.fori_loop(0, SLOTS + 1, clear, 0)
    for n in range(REACH):

        def note(r, carry):
            found[tags[n, r]] = starts[n] + TAG_ROWS + r * FEATURES
            return carry

        lax.fori_loop(0, sources[n][3], note, 0, unroll=10)
    head = lift[...]
    copies = []
    for lat in range(LAT_DEV):
        for col in range(0, COL_BLOCKS, 2):
            tag = lat * COL_BLOCKS + col + 1
            rows = jnp.concatenate(
                [
                    packs[pl.ds(pl.multiple_of(found[tag + n], 16), FEATURES), :]
                    for n in range(2)
                ],
                axis=1,
            )
            value = jnp.dot(
                head, jnp.concatenate([rows, rows], axis=0), preferred_element_type=F32
            )
            work[:, lat, :, col * BLOCK : (col + 2) * BLOCK] = value.reshape(
                FIELDS, LEVELS, 2 * BLOCK
            )
        copies.append(
            pltpu.make_async_copy(work.at[:, lat], out.at[:, lat], out_sems.at[lat])
        )
        copies[-1].start()
    done[...] = jnp.zeros_like(done)
    for copy in copies:
        copy.wait()


def call(kernel, ins, outs, shapes, scratch, name, flops, limit=22, aliases={}):
    return pl.pallas_call(
        kernel,
        in_specs=ins,
        out_specs=outs,
        out_shape=[jax.ShapeDtypeStruct(s, d) for s, d in shapes],
        scratch_shapes=scratch,
        name=name,
        input_output_aliases=aliases,
        cost_estimate=pl.CostEstimate(flops=flops, bytes_accessed=4 * MIB, transcendentals=0),
        compiler_params=pltpu.CompilerParams(vmem_limit_bytes=limit * MIB),
    )


def payloads(far, targets, blocks, order_pairs, arrival, weights):
    part_count = REACH * LAT_DEV + 1
    return call(
        functools.partial(payload_kernel, far),
        [HBM] * 5,
        [VMEM, VMEM] + [HBM] * 4,
        [((part_count, FEATURES, 2 * BLOCK), F32), ((part_count, FEATURES, BLOCK), F32)]
        + [((rows, BLOCK), BF16) for rows in (PACK, PACK, pack_rows(far), 3 * pack_rows(far))],
        [
            pltpu.SMEM((SLOTS,), jnp.int32),
            pltpu.SMEM((SLOTS,), jnp.int32),
            pltpu.SMEM((BANDS,), jnp.int32),
            pltpu.VMEM((FIELDS, LAT_DEV, LEVELS, LONGITUDES), BF16),
            pltpu.VMEM((SLOTS, BLOCK, BLOCK), BF16),
            pltpu.VMEM((2 * BLOCK, 2 * BLOCK), BF16),
            pltpu.VMEM((2, 24, BLOCK), F32),
            pltpu.VMEM((REACH * PACK, BLOCK), BF16),
            pltpu.VMEM((REACH, TAG_ROWS, BLOCK), F32),
            pltpu.VMEM((SLOTS * FEATURES, 2 * BLOCK), BF16),
            pltpu.VMEM((SLOTS * FEATURES, 2 * BLOCK), F32),
            pltpu.SMEM((8,), jnp.int32),
            pltpu.SemaphoreType.DMA((3,)),
            pltpu.SemaphoreType.DMA((2 * LAT_DEV,)),
            pltpu.SemaphoreType.DMA((5,)),
        ],
        "payload_and_part_fourier",
        3 * 10**9,
        36,
    )(targets, blocks, order_pairs, arrival, weights)


def grid_solve(far, lift, kept, pair, hop_all, passed):
    return call(
        functools.partial(grid_kernel, far),
        [VMEM] + [ANY] * 4,
        [HBM, VMEM],
        [((FIELDS, LAT_DEV, LEVELS, LONGITUDES), F32), ((8, BLOCK), F32)],
        [
            pltpu.VMEM((2 * PACK + 3 * pack_rows(far), BLOCK), BF16),
            pltpu.VMEM((FIELDS, LAT_DEV, LEVELS, LONGITUDES), F32),
            pltpu.VMEM((8, BLOCK), jnp.int32),
            pltpu.SMEM((8, BLOCK), jnp.int32),
            pltpu.SMEM((SLOTS + 1,), jnp.int32),
            pltpu.SemaphoreType.DMA((REACH,)),
            pltpu.SemaphoreType.DMA,
            pltpu.SemaphoreType.DMA((LAT_DEV,)),
        ],
        "grid_vertical_solve",
        2 * 10**9,
    )(lift, kept, pair, hop_all, passed)


SWAP = [(b, b ^ 1) for b in range(BANDS)]
HOP = [(b, b + 1) for b in range(1, BANDS - 1, 2)] + [(b, b - 1) for b in range(2, BANDS, 2)]


def on_device(
    arrival_adj, block_weights, dest_band, dest_block, lower_coef, upper_coef, order_pairs, legendre
):
    arrival = arrival_adj.transpose(0, 2, 1, 3)
    weights = block_weights.reshape(SLOTS, BLOCK, BLOCK)
    targets = dest_band.reshape(SLOTS)
    blocks = dest_block.reshape(SLOTS)
    sums, other, kept, pair, transit, hop_own = payloads(
        FAR, targets, blocks, order_pairs, arrival, weights
    )
    other = lax.ppermute(other, "band", SWAP)
    transit = lax.ppermute(transit, "band", SWAP)
    lifts, lift, own = call(
        solve_kernel,
        [HBM, HBM, VMEM],
        [VMEM] * 3,
        [
            ((2 * BLOCK, 4 * BLOCK), BF16),
            ((FEATURES, BLOCK), BF16),
            ((REACH * LAT_DEV + 1, FEATURES, BLOCK), F32),
        ],
        [
            pltpu.VMEM((FIELDS, LEVELS), F32),
            pltpu.VMEM((FIELDS, LEVELS), F32),
            pltpu.VMEM((FEATURES, BLOCK), F32),
            pltpu.SemaphoreType.DMA((2,)),
        ],
        "inverse_of_vertical_operator",
        10**9,
    )(lower_coef, upper_coef, sums)
    message, hop_all = call(
        spread_kernel,
        [VMEM] * 3 + [HBM, ANY],
        [VMEM, HBM],
        [((CHIPS * GROUPS, 16, BLOCK), BF16), ((3 * pack_rows(FAR), BLOCK), BF16)],
        [
            pltpu.VMEM((3840, BLOCK), BF16),
            pltpu.VMEM((CHIPS * GROUPS * 16, BLOCK), F32),
            pltpu.SemaphoreType.DMA,
        ],
        "vertical_solve_of_fourier",
        10**9,
        aliases={3: 1},
    )(own, other, lifts, hop_own, transit)
    message, hop_all, pair = lax.optimization_barrier((message, hop_all, pair))
    hop_all = lax.ppermute(hop_all, "band", HOP)
    pair = lax.ppermute(pair, "band", SWAP)
    same_core = [
        [(chip * 2 + core) * GROUPS + s for chip in range(CHIPS) for s in range(GROUPS)]
        for core in range(2)
    ]
    parts = lax.all_to_all(
        message, ("band", "lev"), split_axis=0, concat_axis=0, axis_index_groups=same_core, tiled=True
    )
    passed = lax.ppermute(hop_all[pack_rows(FAR) : 2 * pack_rows(FAR)], "band", SWAP)
    grid_adj, grid_done = grid_solve(FAR, lift, kept, pair, hop_all, passed)
    spectral, overflow = call(
        legendre_kernel,
        [HBM, ANY, HBM, ANY, ANY],
        [VMEM, SMEM],
        [((2, LEVELS, ORDERS + 1), F32), ((1, 1), F32)],
        [
            pltpu.SMEM((BANDS,), jnp.int32),
            pltpu.VMEM((CHIPS * GROUPS, 16, BLOCK), BF16),
            pltpu.VMEM((CHIPS * GROUPS * 16, BLOCK), F32),
            pltpu.VMEM((LATITUDES, BLOCK), F32),
            pltpu.VMEM((ORDERS, LATITUDES), BF16),
            pltpu.VMEM((1, LATITUDES), BF16),
            pltpu.SemaphoreType.DMA,
            pltpu.SemaphoreType.DMA,
            pltpu.SemaphoreType.DMA((6,)),
        ],
        "legendre_analysis",
        2 * 10**9,
        56,
    )(order_pairs, parts, legendre[0].T, legendre[0, :, ORDERS][None], grid_done)

    def wide_exchange(state):
        _, kept, pair, transit, hop = payloads(
            CAP, targets, blocks, order_pairs, arrival, weights
        )[1:]
        pair = lax.ppermute(pair, "band", SWAP)
        transit = lax.ppermute(transit, "band", SWAP)
        hop = lax.ppermute(jnp.concatenate([hop[: 2 * PACK], transit]), "band", HOP)
        passed = lax.ppermute(hop[PACK : 2 * PACK], "band", SWAP)
        return (jnp.float32(0.0), grid_solve(CAP, lift, kept, pair, hop, passed)[0])

    _, grid_adj = lax.while_loop(
        lambda state: state[0] > 0.0, wide_exchange, (overflow[0, 0], grid_adj)
    )
    return (grid_adj.transpose(0, 2, 1, 3), spectral.transpose(2, 0, 1)[None])


def solution(mesh):
    in_specs = (
        P(None, None, ("band", "lev"), None),
        P("band", "lev", None, None, None),
        P("band", "lev", None),
        P("band", "lev", None),
        P(),
        P(),
        P(),
        P("band", None, None),
    )
    out_specs = (P(None, None, ("band", "lev"), None), P("band", None, None, "lev"))
    return jax.shard_map(
        on_device, mesh=mesh, in_specs=in_specs, out_specs=out_specs, check_vma=False
    )
```

```python
import functools
import math

import jax
import jax.numpy as jnp
from jax import lax
from jax.experimental import pallas as pl
from jax.experimental.pallas import tpu as pltpu
from jax.sharding import PartitionSpec as P

FIELDS = 4
LEVELS = 16
FEATURES = 64
LONGITUDES = 2560
ORDERS = 1280
LAT_DEV = 5
BANDS = 64
GROUPS = 4
CHIPS = 32
REACH = 5
CAP = 40
FAR = 20
BLOCK = 128
TAG_ROWS = 16
PACK = TAG_ROWS + CAP * FEATURES
UNROLL = 20
AHEAD = 2
SLOTS = 100
COL_BLOCKS = 20
LATITUDES = 1280
MIB = 1 << 20
F32 = jnp.float32
BF16 = jnp.bfloat16
VMEM = pl.BlockSpec(memory_space=pltpu.VMEM)
SMEM = pl.BlockSpec(memory_space=pltpu.SMEM)
HBM = pl.BlockSpec(memory_space=pltpu.HBM)
ANY = pl.BlockSpec(memory_space=pl.ANY)


def iota(shape, dim):
    return lax.broadcasted_iota(jnp.int32, shape, dim)


def turned(steps):
    steps = steps - LONGITUDES * jnp.floor((steps + 0.5) * (1.0 / LONGITUDES))
    away = jnp.abs(steps - ORDERS)
    near = jnp.minimum(away, ORDERS - away)
    angle = near * (math.pi / ORDERS)
    t = angle * angle
    value = -1.0 / 87178291200.0
    for term in (479001600.0, -3628800.0, 40320.0, -720.0, 24.0, -2.0, 1.0):
        value = value * t + 1.0 / term
    return jnp.where(away > ORDERS // 2, value, -value)


def solve_rows(below, diagonal, above, start):
    ratios, values = [], []
    for k in range(LEVELS):
        if k == 0:
            inverse = 1.0 / diagonal[0]
            values.append(start[0] * inverse)
        else:
            inverse = 1.0 / (diagonal[k] - below[k] * ratios[k - 1])
            values.append((start[k] - below[k] * values[k - 1]) * inverse)
        ratios.append(above[k] * inverse if k < LEVELS - 1 else None)
    for k in range(LEVELS - 2, -1, -1):
        values[k] = values[k] - ratios[k] * values[k + 1]
    return values


def write_tables(orders, core, inner_table, angles):
    lane = iota((8, BLOCK), 1)
    slot = (lane & 31) * 2 + jnp.where(lane < 64, core, 1 - core)
    order = jnp.zeros((8, BLOCK), jnp.int32)
    for p in range(BANDS):
        order = jnp.where(slot == p, orders[p], order)
    order = jnp.where((lane & 32) == 0, order, ORDERS - 1 - order).astype(F32)[0:1]
    three_quarters = 3.0 * (LONGITUDES // 4)
    inner = iota((BLOCK, BLOCK), 0).astype(F32) * order
    for part, full in enumerate((turned(inner), turned(inner + three_quarters))):
        head = full.astype(BF16)
        cols = slice(part * BLOCK, (part + 1) * BLOCK)
        inner_table[0:BLOCK, cols] = head
        inner_table[BLOCK:, cols] = (full - head.astype(F32)).astype(BF16)
    scale = 1.0 / math.sqrt(LONGITUDES)
    outer = iota((24, BLOCK), 0).astype(F32) * (BLOCK * order)
    angles[0] = turned(outer) * scale
    angles[1] = turned(outer + three_quarters) * scale


def solve_kernel(lower_in, upper_in, sums, lifts, lift_ref, own_part, lower_ref, upper_ref, work, sems):
    loads = [
        pltpu.make_async_copy(lower_in, lower_ref, sems.at[0]),
        pltpu.make_async_copy(upper_in, upper_ref, sems.at[1]),
    ]
    for load in loads:
        load.start()
    half = iota((FEATURES, BLOCK), 1) < 64

    def split(at, carry):
        real = sums[at, :, :BLOCK]
        imaginary = sums[at, :, BLOCK:]
        own_part[at] = jnp.where(half, real, pltpu.roll(imaginary, 64, 1))
        return carry

    lax.fori_loop(0, REACH * LAT_DEV + 1, split, 0, unroll=13)
    for load in loads:
        load.wait()
    lower, upper = lower_ref[...], upper_ref[...]
    lows = [jnp.broadcast_to(lower[:, k : k + 1], (FIELDS, BLOCK)) for k in range(LEVELS)]
    ups = [jnp.broadcast_to(upper[:, k : k + 1], (FIELDS, BLOCK)) for k in range(LEVELS)]
    diagonal = [1.0 + lows[k] + ups[k] for k in range(LEVELS)]
    col = iota((FIELDS, BLOCK), 1)
    mine = ((col >> 4) & 3) == iota((FIELDS, BLOCK), 0)
    zero = jnp.zeros((FIELDS, BLOCK), F32)
    unit = [jnp.where((col & 15) == k, 1.0, 0.0) for k in range(LEVELS)]
    shift_down = [zero] + [-ups[k - 1] for k in range(1, LEVELS)]
    shift_up = [-lows[k + 1] for k in range(LEVELS - 1)] + [zero]
    rows = solve_rows(shift_down, diagonal, shift_up, unit)
    for k in range(LEVELS):
        work[pl.ds(k, FIELDS, stride=LEVELS), :] = jnp.where(mine, rows[k], 0.0)
    full = work[...]
    head = full.astype(BF16).astype(F32)
    lift_ref[...] = jnp.where(iota((FEATURES, BLOCK), 1) < FEATURES, head, full - head).astype(BF16)
    plain_down = [zero] + [-lows[k] for k in range(1, LEVELS)]
    plain_up = [-ups[k] for k in range(LEVELS - 1)] + [zero]
    rows = solve_rows(plain_down, diagonal, plain_up, unit)
    for k in range(LEVELS):
        work[pl.ds(k, FIELDS, stride=LEVELS), :] = rows[k]
    wide = jnp.concatenate([work[...]] * FIELDS, axis=1)
    owned = (iota(wide.shape, 0) >> 4) == (iota(wide.shape, 1) >> 7)
    full = jnp.where(owned, wide, 0.0)
    head = full.astype(BF16)
    lifts[0:64] = head
    lifts[64:128] = head
    lifts[128:192] = (full - head.astype(F32)).astype(BF16)
    lifts[192:256] = jnp.zeros_like(head)


def block_row(block):
    return (
        (block >= 20).astype(jnp.int32)
        + (block >= 40).astype(jnp.int32)
        + (block >= 60).astype(jnp.int32)
        + (block >= 80).astype(jnp.int32)
    )


def pack_rows(cap):
    return TAG_ROWS + cap * FEATURES


def payload_kernel(
    far, dest_band_in, dest_block_in, orders_in, arrival_in, weights_in,
    sums, other_part, kept, pair_out, transit_out, hop_out,
    dest_band, dest_block, orders, arrival, weights, inner_table, angles, packs, tags, line, waves,
    counts, small_sems, in_sems, out_sems,
):
    band = lax.axis_index("band")
    core = lax.rem(band, 2)
    small = [
        pltpu.make_async_copy(source, held, small_sems.at[n])
        for n, (source, held) in enumerate(
            ((orders_in, orders), (dest_band_in, dest_band), (dest_block_in, dest_block))
        )
    ]
    for copy in small:
        copy.start()
    loads = []
    for lat in range(LAT_DEV):
        part = pl.ds(lat * COL_BLOCKS, COL_BLOCKS)
        loads.append(
            (
                pltpu.make_async_copy(arrival_in.at[:, lat], arrival.at[:, lat], in_sems.at[2 * lat]),
                pltpu.make_async_copy(weights_in.at[part], weights.at[part], in_sems.at[2 * lat + 1]),
            )
        )
    for ahead in range(AHEAD):
        for load in loads[ahead]:
            load.start()
    far_rows = pack_rows(far)
    for g in range(REACH):
        counts[g] = 0
    tags[...] = jnp.zeros_like(tags)
    sums[...] = jnp.zeros_like(sums)
    for copy in small:
        copy.wait()
    write_tables(orders, core, inner_table, angles)
    lane = iota((TAG_ROWS, BLOCK), 1)

    def weigh(col, lat):
        j = lat * COL_BLOCKS + col
        rows = arrival[:, lat, :, pl.ds(pl.multiple_of(col * BLOCK, BLOCK), BLOCK)]
        payload = jnp.dot(
            rows.reshape(FEATURES, BLOCK), weights[j], preferred_element_type=F32
        ).astype(BF16)
        line[pl.ds(pl.multiple_of(j * FEATURES, FEATURES), FEATURES), :] = jnp.concatenate(
            [payload, payload], axis=1
        )
        g = dest_band[j] - band + 2
        rank = counts[g]
        counts[g] = rank + 1
        start = pl.multiple_of(g * PACK + TAG_ROWS + rank * FEATURES, 16)
        packs[pl.ds(start, FEATURES), :] = payload
        tag = (dest_block[j] + 1).astype(F32)
        tags[g] = jnp.where(lane == rank, tag, tags[g])
        return lat

    def ship(group, size, out, at, n):
        source = packs.at[pl.ds(pl.multiple_of(group * PACK, 16), size)]
        return pltpu.make_async_copy(source, out.at[pl.ds(at, size)], out_sems.at[n])

    shipped = [
        ship(4 - 4 * core, far_rows, transit_out, 0, 1),
        ship(1 + 2 * core, far_rows, hop_out, 0, 2),
        ship(4 * core, far_rows, hop_out, far_rows, 3),
        ship(3 - 2 * core, PACK, pair_out, 0, 0),
        ship(2, PACK, kept, 0, 4),
    ]

    def transform(lat):
        rows = pl.ds(lat * COL_BLOCKS * FEATURES, COL_BLOCKS * FEATURES)
        waves[rows, :] = jnp.dot(line[rows, :], inner_table[...], preferred_element_type=F32)

    def analyse(j, carry):
        rows = pl.ds(pl.multiple_of(j * FEATURES, FEATURES), FEATURES)
        block = dest_block[j]
        lat = block_row(block)
        at = (dest_band[j] - band + 2) * LAT_DEV + lat
        col = block - lat * COL_BLOCKS
        cosine = angles[0, pl.ds(col, 1), :]
        sine = angles[1, pl.ds(col, 1), :]
        even = waves[rows, :BLOCK]
        odd = waves[rows, BLOCK:]
        sums[at, :, :BLOCK] = sums[at, :, :BLOCK] + (even * cosine - odd * sine)
        sums[at, :, BLOCK:] = sums[at, :, BLOCK:] - (even * sine + odd * cosine)
        return carry

    for lat in range(LAT_DEV):
        for load in loads[lat]:
            load.wait()
        if lat + AHEAD < LAT_DEV:
            for load in loads[lat + AHEAD]:
                load.start()
        lax.fori_loop(0, COL_BLOCKS, weigh, lat, unroll=UNROLL)
        if lat == LAT_DEV - 1:
            for g in range(REACH):
                packs[g * PACK : g * PACK + TAG_ROWS, :] = tags[g].astype(BF16)
            for copy in shipped:
                copy.start()
        transform(lat)
        lax.fori_loop(COL_BLOCKS * lat, COL_BLOCKS * (lat + 1), analyse, 0, unroll=UNROLL)
    longest = jnp.maximum(
        jnp.maximum(counts[4 - 4 * core], counts[1 + 2 * core]), counts[4 * core]
    )
    overflow = jnp.where(longest > far, 1.0, 0.0)
    sums[REACH * LAT_DEV] = jnp.full((FEATURES, 2 * BLOCK), overflow, F32)
    half = iota((FEATURES, BLOCK), 1) < 64

    def split(at, carry):
        real = sums[at, :, :BLOCK]
        imaginary = sums[at, :, BLOCK:]
        other_part[at] = jnp.where(half, pltpu.roll(real, 64, 1), imaginary)
        return carry

    lax.fori_loop(0, REACH * LAT_DEV + 1, split, 0, unroll=13)
    for copy in shipped:
        copy.wait()


def spread_kernel(
    own, other, lifts, hop_own, transit, out, hop_out, turned_rows, work, sem
):
    core = lax.rem(lax.axis_index("band"), 2)
    far_rows = transit.shape[0]
    carry = pltpu.make_async_copy(
        transit, hop_out.at[pl.ds(2 * far_rows, far_rows)], sem
    )
    carry.start()
    for near in range(6):
        for i in range(LAT_DEV):
            if near == 0:
                total = jnp.where(core == 0, own[i], other[i])
            elif near == 5:
                total = jnp.where(core == 1, own[20 + i], other[20 + i])
            else:
                total = own[(near - core) * LAT_DEV + i] + other[(near - 1 + core) * LAT_DEV + i]
            head = total.astype(BF16).astype(F32)
            flipped = jnp.concatenate([head, total - head], axis=0).T.astype(BF16)
            at = ((near // 2) * LAT_DEV + i) * 8 + (near % 2) * 4
            turned_rows[at * 32 : (at + 4) * 32, :] = flipped
    group = (iota((32, 4 * BLOCK), 1) & (BLOCK - 1)) >> 4
    for chunk in range(5):
        part = turned_rows[chunk * 768 : (chunk + 1) * 768, :]
        raised = jnp.dot(
            jnp.concatenate([part, part], axis=1), lifts[...], preferred_element_type=F32
        )
        for r in range(3):
            total = raised[r * 256 : r * 256 + 32]
            for q in range(1, 8):
                low = r * 256 + q * 32
                total = jnp.where(group == q, raised[low : low + 32], total)
            for g in range(GROUPS):
                work[pl.ds(g * 16 + chunk * 3 + r, 32, stride=64), :] = total[
                    :, g * BLOCK : (g + 1) * BLOCK
                ]
    last = REACH * LAT_DEV
    overflow = jnp.maximum(own[last, 0:32, :], other[last, 0:32, :])
    for g in range(GROUPS):
        work[pl.ds(g * 16 + 15, 32, stride=64), :] = overflow
    out[...] = work[...].astype(BF16).reshape(out.shape)
    carry.wait()


def legendre_kernel(
    orders_in, parts_in, legendre_in, grid_done, out, overflow,
    orders, parts, work, gathered, legendre, order_sem, part_sem, load_sem,
):
    fetch = pltpu.make_async_copy(orders_in, orders, order_sem)
    fetch.start()
    bring = pltpu.make_async_copy(parts_in, parts, part_sem)
    bring.start()
    load = pltpu.make_async_copy(legendre_in, legendre, load_sem)
    load.start()
    fetch.wait()
    first = ORDERS - orders[lax.axis_index("band")]
    bring.wait()
    work[...] = parts[...].astype(F32).reshape(work.shape)
    flags = work[pl.ds(15, CHIPS * GROUPS, stride=16), :]
    overflow[0, 0] = jnp.max(flags)
    for chip in range(CHIPS):
        for s in range(GROUPS):
            base = (chip * GROUPS + s) * 16
            total = work[base + 5 : base + 10, :]
            if chip > 0:
                total = total + work[base - 64 + 10 : base - 64 + 15, :]
            if chip < CHIPS - 1:
                total = total + work[base + 64 : base + 64 + 5, :]
            at = chip * 40 + s * LAT_DEV
            gathered[at : at + LAT_DEV, :] = total
            gathered[at + 20 : at + 20 + LAT_DEV, :] = pltpu.roll(total, 64, 1)
    right = gathered[...].astype(BF16)
    load.wait()
    step = 256
    for low in range(0, ORDERS + 1, step):
        size = min(step, ORDERS + 1 - low)
        mixed = jnp.dot(legendre[low : low + size, :], right, preferred_element_type=F32).T
        degree = low + iota((16, size), 1)
        for r in range(2):
            picked = jnp.where(
                degree < first, mixed[r * 32 : r * 32 + 16], mixed[r * 32 + 16 : r * 32 + 32]
            )
            out[r, :, low : low + size] = picked


def grid_kernel(far, lift, kept, pair_in, hop_in, passed, *refs):
    out, done, packs, work, tag_rows, tags, found, in_sems, tag_sem, out_sems = refs
    far_rows = pack_rows(far)
    sources = [
        (kept, 0, PACK, CAP),
        (pair_in, 0, PACK, CAP),
        (hop_in, 0, far_rows, far),
        (hop_in, 2 * far_rows, far_rows, far),
        (passed, 0, far_rows, far),
    ]
    starts = [0, PACK, 2 * PACK, 2 * PACK + far_rows, 2 * PACK + 2 * far_rows]
    loads = [
        pltpu.make_async_copy(
            source.at[pl.ds(low, size)], packs.at[pl.ds(starts[n], size)], in_sems.at[n]
        )
        for n, (source, low, size, _) in enumerate(sources)
    ]
    for load in loads:
        load.start()
    for load in loads:
        load.wait()
    for n in range(REACH):
        row = packs[starts[n] : starts[n] + TAG_ROWS, :]
        tag_rows[n : n + 1, :] = row.astype(F32)[0:1].astype(jnp.int32)
    copy = pltpu.make_async_copy(tag_rows, tags, tag_sem)
    copy.start()
    copy.wait()

    def clear(n, carry):
        found[n] = TAG_ROWS
        return carry

    lax.fori_loop(0, SLOTS + 1, clear, 0)
    for n in range(REACH):

        def note(r, carry):
            found[tags[n, r]] = starts[n] + TAG_ROWS + r * FEATURES
            return carry

        lax.fori_loop(0, sources[n][3], note, 0, unroll=10)
    head = lift[...]
    copies = []
    for lat in range(LAT_DEV):
        for col in range(0, COL_BLOCKS, 2):
            tag = lat * COL_BLOCKS + col + 1
            rows = jnp.concatenate(
                [
                    packs[pl.ds(pl.multiple_of(found[tag + n], 16), FEATURES), :]
                    for n in range(2)
                ],
                axis=1,
            )
            value = jnp.dot(
                head, jnp.concatenate([rows, rows], axis=0), preferred_element_type=F32
            )
            work[:, lat, :, col * BLOCK : (col + 2) * BLOCK] = value.reshape(
                FIELDS, LEVELS, 2 * BLOCK
            )
        copies.append(
            pltpu.make_async_copy(work.at[:, lat], out.at[:, lat], out_sems.at[lat])
        )
        copies[-1].start()
    done[...] = jnp.zeros_like(done)
    for copy in copies:
        copy.wait()


def call(kernel, ins, outs, shapes, scratch, name, flops, limit=22, aliases={}):
    return pl.pallas_call(
        kernel,
        in_specs=ins,
        out_specs=outs,
        out_shape=[jax.ShapeDtypeStruct(s, d) for s, d in shapes],
        scratch_shapes=scratch,
        name=name,
        input_output_aliases=aliases,
        cost_estimate=pl.CostEstimate(flops=flops, bytes_accessed=4 * MIB, transcendentals=0),
        compiler_params=pltpu.CompilerParams(vmem_limit_bytes=limit * MIB),
    )


def payloads(far, targets, blocks, order_pairs, arrival, weights):
    part_count = REACH * LAT_DEV + 1
    return call(
        functools.partial(payload_kernel, far),
        [HBM] * 5,
        [VMEM, VMEM] + [HBM] * 4,
        [((part_count, FEATURES, 2 * BLOCK), F32), ((part_count, FEATURES, BLOCK), F32)]
        + [((rows, BLOCK), BF16) for rows in (PACK, PACK, pack_rows(far), 3 * pack_rows(far))],
        [
            pltpu.SMEM((SLOTS,), jnp.int32),
            pltpu.SMEM((SLOTS,), jnp.int32),
            pltpu.SMEM((BANDS,), jnp.int32),
            pltpu.VMEM((FIELDS, LAT_DEV, LEVELS, LONGITUDES), BF16),
            pltpu.VMEM((SLOTS, BLOCK, BLOCK), BF16),
            pltpu.VMEM((2 * BLOCK, 2 * BLOCK), BF16),
            pltpu.VMEM((2, 24, BLOCK), F32),
            pltpu.VMEM((REACH * PACK, BLOCK), BF16),
            pltpu.VMEM((REACH, TAG_ROWS, BLOCK), F32),
            pltpu.VMEM((SLOTS * FEATURES, 2 * BLOCK), BF16),
            pltpu.VMEM((SLOTS * FEATURES, 2 * BLOCK), F32),
            pltpu.SMEM((8,), jnp.int32),
            pltpu.SemaphoreType.DMA((3,)),
            pltpu.SemaphoreType.DMA((2 * LAT_DEV,)),
            pltpu.SemaphoreType.DMA((5,)),
        ],
        "payload_and_part_fourier",
        3 * 10**9,
        36,
    )(targets, blocks, order_pairs, arrival, weights)


def grid_solve(far, lift, kept, pair, hop_all, passed):
    return call(
        functools.partial(grid_kernel, far),
        [VMEM] + [ANY] * 4,
        [HBM, VMEM],
        [((FIELDS, LAT_DEV, LEVELS, LONGITUDES), F32), ((8, BLOCK), F32)],
        [
            pltpu.VMEM((2 * PACK + 3 * pack_rows(far), BLOCK), BF16),
            pltpu.VMEM((FIELDS, LAT_DEV, LEVELS, LONGITUDES), F32),
            pltpu.VMEM((8, BLOCK), jnp.int32),
            pltpu.SMEM((8, BLOCK), jnp.int32),
            pltpu.SMEM((SLOTS + 1,), jnp.int32),
            pltpu.SemaphoreType.DMA((REACH,)),
            pltpu.SemaphoreType.DMA,
            pltpu.SemaphoreType.DMA((LAT_DEV,)),
        ],
        "grid_vertical_solve",
        2 * 10**9,
    )(lift, kept, pair, hop_all, passed)


SWAP = [(b, b ^ 1) for b in range(BANDS)]
HOP = [(b, b + 1) for b in range(1, BANDS - 1, 2)] + [(b, b - 1) for b in range(2, BANDS, 2)]


def on_device(
    arrival_adj, block_weights, dest_band, dest_block, lower_coef, upper_coef, order_pairs, legendre
):
    arrival = arrival_adj.transpose(0, 2, 1, 3)
    weights = block_weights.reshape(SLOTS, BLOCK, BLOCK)
    targets = dest_band.reshape(SLOTS)
    blocks = dest_block.reshape(SLOTS)
    sums, other, kept, pair, transit, hop_own = payloads(
        FAR, targets, blocks, order_pairs, arrival, weights
    )
    other = lax.ppermute(other, "band", SWAP)
    transit = lax.ppermute(transit, "band", SWAP)
    lifts, lift, own = call(
        solve_kernel,
        [HBM, HBM, VMEM],
        [VMEM] * 3,
        [
            ((2 * BLOCK, 4 * BLOCK), BF16),
            ((FEATURES, BLOCK), BF16),
            ((REACH * LAT_DEV + 1, FEATURES, BLOCK), F32),
        ],
        [
            pltpu.VMEM((FIELDS, LEVELS), F32),
            pltpu.VMEM((FIELDS, LEVELS), F32),
            pltpu.VMEM((FEATURES, BLOCK), F32),
            pltpu.SemaphoreType.DMA((2,)),
        ],
        "inverse_of_vertical_operator",
        10**9,
    )(lower_coef, upper_coef, sums)
    message, hop_all = call(
        spread_kernel,
        [VMEM] * 3 + [HBM, ANY],
        [VMEM, HBM],
        [((CHIPS * GROUPS, 16, BLOCK), BF16), ((3 * pack_rows(FAR), BLOCK), BF16)],
        [
            pltpu.VMEM((3840, BLOCK), BF16),
            pltpu.VMEM((CHIPS * GROUPS * 16, BLOCK), F32),
            pltpu.SemaphoreType.DMA,
        ],
        "vertical_solve_of_fourier",
        10**9,
        aliases={3: 1},
    )(own, other, lifts, hop_own, transit)
    message, hop_all, pair = lax.optimization_barrier((message, hop_all, pair))
    hop_all = lax.ppermute(hop_all, "band", HOP)
    pair = lax.ppermute(pair, "band", SWAP)
    same_core = [
        [(chip * 2 + core) * GROUPS + s for chip in range(CHIPS) for s in range(GROUPS)]
        for core in range(2)
    ]
    parts = lax.all_to_all(
        message, ("band", "lev"), split_axis=0, concat_axis=0, axis_index_groups=same_core, tiled=True
    )
    passed = lax.ppermute(hop_all[pack_rows(FAR) : 2 * pack_rows(FAR)], "band", SWAP)
    grid_adj, grid_done = grid_solve(FAR, lift, kept, pair, hop_all, passed)
    spectral, overflow = call(
        legendre_kernel,
        [HBM, ANY, HBM, ANY],
        [VMEM, SMEM],
        [((2, LEVELS, ORDERS + 1), F32), ((1, 1), F32)],
        [
            pltpu.SMEM((BANDS,), jnp.int32),
            pltpu.VMEM((CHIPS * GROUPS, 16, BLOCK), BF16),
            pltpu.VMEM((CHIPS * GROUPS * 16, BLOCK), F32),
            pltpu.VMEM((LATITUDES, BLOCK), F32),
            pltpu.VMEM((ORDERS + 1, LATITUDES), BF16),
            pltpu.SemaphoreType.DMA,
            pltpu.SemaphoreType.DMA,
            pltpu.SemaphoreType.DMA,
        ],
        "legendre_analysis",
        2 * 10**9,
        56,
    )(order_pairs, parts, legendre[0].T, grid_done)

    def wide_exchange(state):
        _, kept, pair, transit, hop = payloads(
            CAP, targets, blocks, order_pairs, arrival, weights
        )[1:]
        pair = lax.ppermute(pair, "band", SWAP)
        transit = lax.ppermute(transit, "band", SWAP)
        hop = lax.ppermute(jnp.concatenate([hop[: 2 * PACK], transit]), "band", HOP)
        passed = lax.ppermute(hop[PACK : 2 * PACK], "band", SWAP)
        return (jnp.float32(0.0), grid_solve(CAP, lift, kept, pair, hop, passed)[0])

    _, grid_adj = lax.while_loop(
        lambda state: state[0] > 0.0, wide_exchange, (overflow[0, 0], grid_adj)
    )
    return (grid_adj.transpose(0, 2, 1, 3), spectral.transpose(2, 0, 1)[None])


def solution(mesh):
    in_specs = (
        P(None, None, ("band", "lev"), None),
        P("band", "lev", None, None, None),
        P("band", "lev", None),
        P("band", "lev", None),
        P(),
        P(),
        P(),
        P("band", None, None),
    )
    out_specs = (P(None, None, ("band", "lev"), None), P("band", None, None, "lev"))
    return jax.shard_map(
        on_device, mesh=mesh, in_specs=in_specs, out_specs=out_specs, check_vma=False
    )
```
